256 devices in a mesh: gx: 8 (over x, core), gy: 4 (over y), gz: 8 (over z).
Axes of the slice: x: 4, y: 4, z: 8, core: 2. Of those that a mesh axis runs over, the one named last changes fastest.
Arguments:
- attributes: bfloat16 [32, 64, 32, 1024], P(None, 'gx', 'gy', 'gz'), may hold values from -11 to 11, as said below
- start_centroids: float32 [32, 32], replicated, may hold values from -6 to 6
Outputs:
- centroids: float32 [32, 32], replicated
- memberships: float32 [32, 64, 32, 1024], P(None, 'gx', 'gy', 'gz')
The draws below stay inside these ranges and needn't reach their ends.
Inputs may be any that keep to these rules, and one draw needn't show every extreme that they name: `attributes`: each voxel's attribute values.
All inputs are finite; a program needn't handle non-finite values.
Results may differ from the reference program's by a relative error of at most 0.011.
Values may be sent and summed in bfloat16 or wider, within the bound.
No kernel may reach another device: no remote copies, remote signals or barrier semaphores. Data moves between devices by JAX's collectives and lax.ppermute only.
A program may use at most 64 MiB of HBM per device.

```python
import math
import jax
import jax.numpy as jnp
from jax import lax

ATTR = 32
FACIES = 32
UPDATES = 2
NX = 64
NY = 32
NZ = 1024


def facies_centres(key):
    inner = jax.random.fold_in(key, 11)
    return jnp.clip(1.5 * jax.random.normal(inner, (FACIES, ATTR), jnp.float32), -4.0, 4.0)


def position_ramp(count):
    return (jnp.arange(count, dtype=jnp.float32) + 0.5) / count - 0.5


def layered_labels(table_key, dip_key):
    patch_x = jnp.arange(NX, dtype=jnp.int32) // 3
    patch_y = jnp.arange(NY, dtype=jnp.int32) // 3
    tiles_x = (NX + 2) // 3
    tiles_y = (NY + 2) // 3
    tiles_z = NZ // 4 + 2
    dips = jax.random.randint(dip_key, (tiles_x, tiles_y), 0, 4)
    column_dip = dips[patch_x[:, None], patch_y[None, :]]
    layer = (jnp.arange(NZ, dtype=jnp.int32)[None, None, :] + column_dip[:, :, None]) // 4
    table = jax.random.randint(table_key, (tiles_x, tiles_y, tiles_z), 0, FACIES)
    return table[patch_x[:, None, None], patch_y[None, :, None], layer]


def draw_attributes(key, part):
    centres = facies_centres(key)
    key = jax.random.fold_in(key, 7)
    first = jax.random.fold_in(key, 0)
    second = jax.random.fold_in(key, 1)
    third = jax.random.fold_in(key, 2)
    fifth = jax.random.fold_in(key, 4)
    sixth = jax.random.fold_in(key, 5)
    labels = layered_labels(third, sixth)
    base = jnp.take(jnp.transpose(centres), labels, axis=1)
    shape = (ATTR, NX, NY, NZ)
    drift_dirs = jnp.clip(jax.random.normal(fifth, (3, ATTR), jnp.float32), -2.0, 2.0)
    ramp_x = position_ramp(NX)[None, :, None, None]
    ramp_y = position_ramp(NY)[None, None, :, None]
    ramp_z = position_ramp(NZ)[None, None, None, :]
    drift = drift_dirs[0][:, None, None, None] * ramp_x + drift_dirs[1][:, None, None, None] * ramp_y + drift_dirs[2][:, None, None, None] * ramp_z
    noise = 0.5 * jnp.clip(jax.random.normal(first, shape, jnp.float32), -4.0, 4.0)
    rough = jnp.exp(jax.random.uniform(second, (1, NX, NY, NZ), jnp.float32, -math.log(2.0), math.log(2.0)))
    return jnp.clip(base + drift + noise * rough, -11.0, 11.0).astype(jnp.bfloat16)


def draw_start_centroids(key, part):
    centres = facies_centres(key)
    key = jax.random.fold_in(key, 5)
    shift = jnp.clip(jax.random.normal(key, (FACIES, ATTR), jnp.float32), -3.0, 3.0)
    return centres + 0.4 * shift


def setup_inputs(seed: int = 0) -> dict:
    key_of = jax.random.split(jax.random.key(seed), 3)
    return {
        "attributes": draw_attributes(jax.random.fold_in(key_of[2], 71), 0),
        "start_centroids": draw_start_centroids(jax.random.fold_in(key_of[2], 71), 0),
    }


def window_sum(padded, dim):
    count = padded.shape[dim] - 4
    total = lax.slice_in_dim(padded, 0, count, axis=dim)
    for shift in range(1, 5):
        total = total + lax.slice_in_dim(padded, shift, shift + count, axis=dim)
    return total


def box_one(field):
    padded = jnp.pad(field.astype(jnp.float32), 2)
    return window_sum(window_sum(window_sum(padded, 0), 1), 2)


def reference(attributes, start_centroids):
    centroids = start_centroids
    values = attributes.astype(jnp.float32)
    squares = jnp.sum(values * values, axis=0)
    memberships = None
    for step in range(UPDATES):
        cb = centroids.astype(jnp.bfloat16).astype(jnp.float32)
        cross = jnp.einsum("ka,axyz->kxyz", cb, values)
        csq = jnp.sum(centroids * centroids, axis=1)
        dist = squares[None] - 2.0 * cross + csq[:, None, None, None] + 1.0
        inverse = 1.0 / dist
        raw = inverse / jnp.sum(inverse, axis=0, keepdims=True)
        rounded = raw.astype(jnp.bfloat16)
        box = lax.map(box_one, rounded)
        product = raw * box
        memberships = product / jnp.sum(product, axis=0, keepdims=True)
        weights = (memberships * memberships).astype(jnp.bfloat16).astype(jnp.float32)
        numer = jnp.einsum("kxyz,axyz->ka", weights, values)
        denom = jnp.sum(weights, axis=(1, 2, 3))
        centroids = numer / denom[:, None]
    return centroids, memberships
```

```python
import functools
import jax
import jax.numpy as jnp
import numpy as np
from jax import lax
from jax.experimental import pallas as pl
from jax.experimental.pallas import tpu as pltpu
from jax.sharding import Mesh, PartitionSpec as P

UPDATES = 2
F = 32
W = 8
E = W + 4
ZT = 12
BF16 = jnp.bfloat16
F32 = jnp.float32
XS = ("cx", "core")


def z_tiles():
    out = []
    for dy in (0, -1, 1):
        for half in (0, 1):
            out.append((0, dy, half))
    for dx, half in ((-1, 1), (1, 0)):
        for dy in (0, -1, 1):
            out.append((dx, dy, half))
    return out


def halo_matrix():
    src = []
    for dx, dy, half in z_tiles():
        for j in range(32):
            c = half * 32 + j
            for t in range(4):
                src.append((dx * W + c // W, dy * W + c % W, (-2, -1, 128, 129)[t]))
    src = np.array(src)
    dst = []
    for c in range(W * W):
        for t in range(4):
            dst.append((c // W, c % W, (126, 127, 0, 1)[t]))
    dst = np.array(dst)
    near = (np.abs(src[:, None, :] - dst[None, :, :]) <= 2).all(-1)
    return near.astype(np.float32)


def band_matrix():
    z = np.arange(128)
    return (np.abs(z[:, None] - z[None, :]) <= 2).astype(np.float32)


def recip(x):
    r = pl.reciprocal(x, approx=True)
    return r * (2.0 - x * r)


def unpack_centroids(packed):
    return jnp.concatenate([packed[:, 32 * g:32 * g + 32] for g in range(4)], axis=0)


def pack_rows(wide):
    return jnp.concatenate([wide[8 * g:8 * g + 8] for g in range(4)], axis=1)


def update_kernel(text, zt, cent, edge, smat, band, memb, part, inv_s, win_s):
    c = unpack_centroids(cent[0:8, :] / cent[8:16, :])
    cbm2 = (-2.0 * c.astype(BF16).astype(F32)).astype(BF16)
    csq1 = jnp.broadcast_to(jnp.sum(c * c, axis=1, keepdims=True) + 1.0, (F, 128))
    xlo, xhi, ylo, yhi, zlo, zhi = [edge[i] for i in range(6)]

    def inverse(a):
        af = a.astype(F32)
        sq = jnp.sum(af * af, axis=0, keepdims=True)
        cross = jnp.dot(cbm2, a, preferred_element_type=F32)
        n = a.shape[1] // 128
        parts = []
        for i in range(n):
            s = slice(128 * i, 128 * i + 128)
            parts.append(recip(cross[:, s] + csq1 + sq[:, s]))
        return parts

    def normalised(inv, mask):
        return (inv * (recip(jnp.sum(inv, axis=0, keepdims=True)) * mask)).astype(BF16)

    def front(X, carry):
        mx = jnp.where(X < 2, xlo, jnp.where(X >= W + 2, xhi, 1.0))
        rounded = []
        for Y in range(0, E, 2):
            pair = jnp.concatenate([text[X * E + Y], text[X * E + Y + 1]], axis=1)
            my = ylo if Y < 2 else (yhi if Y >= W + 2 else None)
            m = mx if my is None else mx * my
            for i, inv in enumerate(inverse(pair)):
                if 2 <= Y < W + 2:
                    inv_s[X * W + Y + i - 2] = inv
                rounded.append(normalised(inv, m))
        rows = jnp.concatenate(rounded, axis=0)
        z = jnp.dot(rows, band[...], preferred_element_type=F32)
        cols = [z[32 * Y:32 * Y + 32] for Y in range(E)]
        p = [cols[Y] + cols[Y + 1] for Y in range(E - 1)]
        for y in range(W):
            win_s[X * W + y] = p[y] + p[y + 2] + cols[y + 4]
        return carry

    lax.fori_loop(0, E, front, 0)

    lane = lax.broadcasted_iota(jnp.int32, (1, 128), 1)
    mz = jnp.where(lane % 4 < 2, zlo, zhi)
    rz = []
    for i, (dx, dy, half) in enumerate(z_tiles()):
        m = mz
        if dx:
            m = m * (xlo if dx < 0 else xhi)
        if dy:
            m = m * (ylo if dy < 0 else yhi)
        rz.append(normalised(inverse(zt[i])[0], m))
    halo = jnp.dot(jnp.concatenate(rz, axis=1), smat[...], preferred_element_type=F32)
    halves = [halo[:, :128], halo[:, 128:]]
    ends = (lane < 2) | (lane >= 126)

    numer = jnp.zeros((F, F), F32)
    denom = jnp.zeros((F, 128), F32)
    for x in range(W):
        ws, ts = [], []
        for y in range(W):
            i = x * W + y
            box = win_s[i]
            for d in range(1, 5):
                box = box + win_s[i + d * W]
            h = pltpu.roll(halves[i // 32], (126 - 4 * (i % 32)) % 128, 1)
            box = box + jnp.where(ends, h, 0.0)
            prod = inv_s[i + 2 * W] * box
            m = prod * recip(jnp.sum(prod, axis=0, keepdims=True))
            memb[i] = m
            w = (m * m).astype(BF16)
            denom = denom + w.astype(F32)
            ws.append(w)
            ts.append(text[(x + 2) * E + y + 2])
        numer = numer + lax.dot_general(
            jnp.concatenate(ws, axis=1), jnp.concatenate(ts, axis=1),
            (((1,), (1,)), ((), ())), preferred_element_type=F32)
    total = jnp.broadcast_to(jnp.sum(denom, axis=1, keepdims=True), (F, F))
    part[0:8, :] = pack_rows(numer)
    part[8:16, :] = pack_rows(total)


def update(text, zt, cent, edge):
    vmem = pl.BlockSpec(memory_space=pltpu.VMEM)
    return pl.pallas_call(
        update_kernel,
        out_shape=(
            jax.ShapeDtypeStruct((W * W, F, 128), F32),
            jax.ShapeDtypeStruct((16, 128), F32),
        ),
        in_specs=[vmem, vmem, vmem, pl.BlockSpec(memory_space=pltpu.SMEM), vmem, vmem],
        out_specs=(vmem, vmem),
        scratch_shapes=[
            pltpu.VMEM((E * W, F, 128), F32),
            pltpu.VMEM((E * W, F, 128), F32),
        ],
        compiler_params=pltpu.CompilerParams(vmem_limit_bytes=40 << 20),
    )(text, zt, cent, edge, jnp.asarray(halo_matrix(), BF16), jnp.asarray(band_matrix(), BF16))


def both_ways(up, down, axes, count):
    lo = lax.ppermute(up, axes, [(i, (i + 1) % count) for i in range(count)])
    hi = lax.ppermute(down, axes, [((i + 1) % count, i) for i in range(count)])
    return lo, hi


def gather_sum(part, axes, count):
    every = lax.all_to_all(jnp.broadcast_to(part[None], (count,) + part.shape), axes, 0, 0)
    return jnp.sum(every, axis=0)


def total_sums(part):
    part = part + lax.ppermute(part, "core", [(0, 1), (1, 0)])
    part = gather_sum(part, ("cx", "gy"), 16)
    return gather_sum(part, ("gz",), 8)


def packed_ends(cols):
    ends = jnp.concatenate([cols[:, :, 126:], cols[:, :, :2]], axis=2)
    return ends.reshape(2, 32, F, 4).transpose(0, 2, 1, 3).reshape(2, F, 128)


def extended(attributes):
    own = attributes.transpose(1, 2, 0, 3)
    ends = packed_ends(own.reshape(W * W, F, 128))
    zlo, zhi = both_ways(ends, ends, "gz", 8)
    lane = lax.broadcasted_iota(jnp.int32, ends.shape, 2)
    zown = jnp.where(lane % 4 < 2, zlo, zhi)

    def y_slice(s):
        return jnp.concatenate([own[:, s].reshape(2 * W, F, 128), zown])

    ylo, yhi = both_ways(y_slice(slice(W - 2, W)), y_slice(slice(0, 2)), "gy", 4)
    zy = [zown, ylo[2 * W:], yhi[2 * W:]]
    middle = jnp.concatenate(
        [ylo[:2 * W].reshape(W, 2, F, 128), own, yhi[:2 * W].reshape(W, 2, F, 128)], axis=1)

    def x_slice(s, half):
        return jnp.concatenate(
            [middle[s].reshape(2 * E, F, 128)] + [z[half:half + 1] for z in zy])

    xlo, xhi = both_ways(x_slice(slice(W - 2, W), 1), x_slice(slice(0, 2), 0), XS, 8)
    text = jnp.concatenate([xlo[:2 * E], middle.reshape(W * E, F, 128), xhi[:2 * E]])
    zt = jnp.concatenate(zy + [xlo[2 * E:], xhi[2 * E:]])
    return text, zt


def edges():
    gx, gy, gz = lax.axis_index(XS), lax.axis_index("gy"), lax.axis_index("gz")
    return jnp.stack([gx > 0, gx < 7, gy > 0, gy < 3, gz > 0, gz < 7]).astype(F32)


def per_device(attributes, start_centroids):
    text, zt = extended(attributes)
    edge = edges()
    packed = jnp.concatenate([start_centroids[8 * g:8 * g + 8] for g in range(4)], axis=1)
    cent = jnp.concatenate([packed, jnp.ones_like(packed)])
    for _ in range(UPDATES):
        memb, part = update(text, zt, cent, edge)
        cent = total_sums(part)
    packed = cent[:8] / cent[8:]
    centroids = jnp.concatenate([packed[:, 32 * g:32 * g + 32] for g in range(4)], axis=0)
    return centroids, memb.reshape(W, W, F, 128).transpose(2, 0, 1, 3)


def solution(mesh):
    split = Mesh(np.asarray(mesh.devices).reshape(4, 2, 4, 8), ("cx", "core", "gy", "gz"))
    placed = (P(None, XS, "gy", "gz"), P())
    return jax.shard_map(
        per_device,
        mesh=split,
        in_specs=placed,
        out_specs=(P(), P(None, XS, "gy", "gz")),
        check_vma=False,
    )
```

```python
import jax
import jax.numpy as jnp
import numpy as np
from jax import lax
from jax.experimental import pallas as pl
from jax.experimental.pallas import tpu as pltpu
from jax.sharding import Mesh, PartitionSpec as P

UPDATES = 2
F = 32
W = 8
E = W + 4
ZT = 12
BF16 = jnp.bfloat16
F32 = jnp.float32
XS = ("cx", "core")


def z_tiles():
    out = []
    for dy in (0, -1, 1):
        for half in (0, 1):
            out.append((0, dy, half))
    for dx, half in ((-1, 1), (1, 0)):
        for dy in (0, -1, 1):
            out.append((dx, dy, half))
    return out


def halo_matrix():
    src = []
    for dx, dy, half in z_tiles():
        for j in range(32):
            c = half * 32 + j
            for t in range(4):
                src.append((dx * W + c // W, dy * W + c % W, (-2, -1, 128, 129)[t]))
    src = np.array(src)
    dst = []
    for c in range(W * W):
        for t in range(4):
            dst.append((c // W, c % W, (126, 127, 0, 1)[t]))
    dst = np.array(dst)
    near = (np.abs(src[:, None, :] - dst[None, :, :]) <= 2).all(-1)
    return near.astype(np.float32)


def band_matrix():
    z = np.arange(128)
    return (np.abs(z[:, None] - z[None, :]) <= 2).astype(np.float32)


def recip(x):
    r = pl.reciprocal(x, approx=True)
    return r * (2.0 - x * r)


def unpacked_centroids(sums):
    lane = lax.broadcasted_iota(jnp.int32, (8, 128), 1)
    row = lax.broadcasted_iota(jnp.int32, (8, 128), 0)
    denom = jnp.broadcast_to(sums[8:9, :], (8, 128))
    parts = []
    for g in range(4):
        d = jnp.sum(jnp.where(lane == row + 8 * g, denom, 0.0), axis=1, keepdims=True)
        parts.append(sums[0:8, 32 * g:32 * g + 32] / d)
    return jnp.concatenate(parts, axis=0)


def pack_rows(wide):
    return jnp.concatenate([wide[8 * g:8 * g + 8] for g in range(4)], axis=1)


def dot_lanes(a, b):
    return lax.dot_general(a, b, (((1,), (1,)), ((), ())), preferred_element_type=F32)


def update_kernel(text, zt, cent, edge, smat, band, memb, part, inv_s, win_s):
    c = unpacked_centroids(cent)
    cbm2 = (-2.0 * c.astype(BF16).astype(F32)).astype(BF16)
    csq1 = jnp.broadcast_to(jnp.sum(c * c, axis=1, keepdims=True) + 1.0, (F, 128))
    xlo, xhi, ylo, yhi, zlo, zhi = [edge[i] for i in range(6)]

    def inverse(a):
        af = a.astype(F32)
        sq = jnp.sum(af * af, axis=0, keepdims=True)
        cross = jnp.dot(cbm2, a, preferred_element_type=F32)
        n = a.shape[1] // 128
        parts = []
        for i in range(n):
            s = slice(128 * i, 128 * i + 128)
            parts.append(recip(cross[:, s] + csq1 + sq[:, s]))
        return parts

    def normalised(inv, mask):
        return (inv * (recip(jnp.sum(inv, axis=0, keepdims=True)) * mask)).astype(BF16)

    def front(X):
        mx = xlo if X < 2 else (xhi if X >= W + 2 else 1.0)
        rounded = []
        for Y in range(0, E, 2):
            pair = jnp.concatenate([text[X * E + Y], text[X * E + Y + 1]], axis=1)
            my = ylo if Y < 2 else (yhi if Y >= W + 2 else None)
            m = mx if my is None else mx * my
            for i, inv in enumerate(inverse(pair)):
                if 2 <= Y < W + 2:
                    inv_s[X * W + Y + i - 2] = inv
                rounded.append(normalised(inv, m))
        rows = jnp.concatenate(rounded, axis=0)
        z = jnp.dot(rows, band[...], preferred_element_type=F32)
        cols = [z[32 * Y:32 * Y + 32] for Y in range(E)]
        p = [cols[Y] + cols[Y + 1] for Y in range(E - 1)]
        for y in range(W):
            win_s[X * W + y] = p[y] + p[y + 2] + cols[y + 4]

    for X in range(E):
        front(X)

    lane = lax.broadcasted_iota(jnp.int32, (1, 128), 1)
    mz = jnp.where(lane % 4 < 2, zlo, zhi)
    rz = []
    for i, (dx, dy, half) in enumerate(z_tiles()):
        m = mz
        if dx:
            m = m * (xlo if dx < 0 else xhi)
        if dy:
            m = m * (ylo if dy < 0 else yhi)
        rz.append(normalised(inverse(zt[i])[0], m))
    halo = jnp.dot(jnp.concatenate(rz, axis=1), smat[...], preferred_element_type=F32)
    halves = [halo[:, :128], halo[:, 128:]]
    ends = (lane < 2) | (lane >= 126)

    numer = jnp.zeros((F, F), F32)
    denom = jnp.zeros((8, F), F32)
    ones = jnp.ones((8, W * 128), BF16)
    for x in range(W):
        ws, ts = [], []
        for y in range(W):
            i = x * W + y
            box = win_s[i]
            for d in range(1, 5):
                box = box + win_s[i + d * W]
            h = pltpu.roll(halves[i // 32], (126 - 4 * (i % 32)) % 128, 1)
            box = box + jnp.where(ends, h, 0.0)
            prod = inv_s[i + 2 * W] * box
            m = prod * recip(jnp.sum(prod, axis=0, keepdims=True))
            memb[i] = m
            w = (m * m).astype(BF16)
            ws.append(w)
            ts.append(text[(x + 2) * E + y + 2])
        w = jnp.concatenate(ws, axis=1)
        numer = numer + dot_lanes(w, jnp.concatenate(ts, axis=1))
        denom = denom + dot_lanes(ones, w)
    part[0:8, :] = pack_rows(numer)
    part[8:9, :] = jnp.concatenate([denom[0:1]] * 4, axis=1)


def update(text, zt, cent, edge):
    vmem = pl.BlockSpec(memory_space=pltpu.VMEM)
    return pl.pallas_call(
        update_kernel,
        out_shape=(
            jax.ShapeDtypeStruct((W * W, F, 128), F32),
            jax.ShapeDtypeStruct((9, 128), F32),
        ),
        in_specs=[vmem, vmem, vmem, pl.BlockSpec(memory_space=pltpu.SMEM), vmem, vmem],
        out_specs=(vmem, vmem),
        scratch_shapes=[
            pltpu.VMEM((E * W, F, 128), F32),
            pltpu.VMEM((E * W, F, 128), F32),
        ],
        compiler_params=pltpu.CompilerParams(vmem_limit_bytes=40 << 20),
    )(text, zt, cent, edge, jnp.asarray(halo_matrix(), BF16), jnp.asarray(band_matrix(), BF16))


def both_ways(up, down, axes, count):
    lo = lax.ppermute(up, axes, [(i, (i + 1) % count) for i in range(count)])
    hi = lax.ppermute(down, axes, [((i + 1) % count, i) for i in range(count)])
    return lo, hi


def gather_sum(part, axes, count):
    every = lax.all_to_all(jnp.broadcast_to(part[None], (count,) + part.shape), axes, 0, 0)
    return jnp.sum(every, axis=0)


def total_sums(part):
    part = part.reshape(9, 1, 128)
    part = part + lax.ppermute(part, "core", [(0, 1), (1, 0)])
    part = gather_sum(part, ("gz",), 8)
    return gather_sum(part, ("cx", "gy"), 16).reshape(9, 128)


def packed_ends(cols):
    ends = jnp.concatenate([cols[:, :, 126:], cols[:, :, :2]], axis=2)
    return ends.reshape(2, 32, F, 4).transpose(0, 2, 1, 3).reshape(2, F, 128)


def extended(attributes):
    own = attributes.transpose(1, 2, 0, 3)
    ends = packed_ends(own.reshape(W * W, F, 128))
    zlo, zhi = both_ways(ends, ends, "gz", 8)
    lane = lax.broadcasted_iota(jnp.int32, ends.shape, 2)
    zown = jnp.where(lane % 4 < 2, zlo, zhi)

    def y_slice(s):
        return jnp.concatenate([own[:, s].reshape(2 * W, F, 128), zown])

    ylo, yhi = both_ways(y_slice(slice(W - 2, W)), y_slice(slice(0, 2)), "gy", 4)
    zy = [zown, ylo[2 * W:], yhi[2 * W:]]
    middle = jnp.concatenate(
        [ylo[:2 * W].reshape(W, 2, F, 128), own, yhi[:2 * W].reshape(W, 2, F, 128)], axis=1)

    def x_slice(s, half):
        return jnp.concatenate(
            [middle[s].reshape(2 * E, F, 128)] + [z[half:half + 1] for z in zy])

    xlo, xhi = both_ways(x_slice(slice(W - 2, W), 1), x_slice(slice(0, 2), 0), XS, 8)
    text = jnp.concatenate([xlo[:2 * E], middle.reshape(W * E, F, 128), xhi[:2 * E]])
    zt = jnp.concatenate(zy + [xlo[2 * E:], xhi[2 * E:]])
    return text, zt


def edges():
    gx, gy, gz = lax.axis_index(XS), lax.axis_index("gy"), lax.axis_index("gz")
    return jnp.stack([gx > 0, gx < 7, gy > 0, gy < 3, gz > 0, gz < 7]).astype(F32)


def per_device(attributes, start_centroids):
    text, zt = extended(attributes)
    edge = edges()
    packed = jnp.concatenate([start_centroids[8 * g:8 * g + 8] for g in range(4)], axis=1)
    cent = jnp.concatenate([packed, jnp.ones((1, 128), F32)])
    for _ in range(UPDATES):
        memb, part = update(text, zt, cent, edge)
        cent = total_sums(part)
    numer = cent[:8].reshape(8, 4, 32).transpose(1, 0, 2).reshape(F, F)
    centroids = numer / cent[8, :F][:, None]
    return centroids, memb.reshape(W, W, F, 128).transpose(2, 0, 1, 3)


def solution(mesh):
    split = Mesh(np.asarray(mesh.devices).reshape(4, 2, 4, 8), ("cx", "core", "gy", "gz"))
    placed = (P(None, XS, "gy", "gz"), P())
    return jax.shard_map(
        per_device,
        mesh=split,
        in_specs=placed,
        out_specs=(P(), P(None, XS, "gy", "gz")),
        check_vma=False,
    )
```

```python
import jax
import jax.numpy as jnp
import numpy as np
from jax import lax
from jax.experimental import pallas as pl
from jax.experimental.pallas import tpu as pltpu
from jax.sharding import Mesh, PartitionSpec as P

F = 32
W = 8
E = W + 4
COLS = W * W
BF16 = jnp.bfloat16
F32 = jnp.float32
XS = ("cx", "core")
OUTER = (0, 1, W - 2, W - 1)
INNER = tuple(range(2, W - 2))


def z_tiles():
    near = [(0, dy, half) for dy in (0, -1, 1) for half in (0, 1)]
    far = [(dx, dy, half) for dx, half in ((-1, 1), (1, 0)) for dy in (0, -1, 1)]
    return near, far


def halo_matrix(tiles):
    src = []
    for dx, dy, half in tiles:
        for c in range(half * 32, half * 32 + 32):
            for t in range(4):
                src.append((dx * W + c // W, dy * W + c % W, (-2, -1, 128, 129)[t]))
    dst = [(c // W, c % W, (126, 127, 0, 1)[t]) for c in range(COLS) for t in range(4)]
    gap = np.abs(np.array(src)[:, None, :] - np.array(dst)[None, :, :])
    return (gap <= 2).all(-1).astype(np.float32)


def band_matrix():
    z = np.arange(128)
    return (np.abs(z[:, None] - z[None, :]) <= 2).astype(np.float32)


def recip(x):
    r = pl.reciprocal(x, approx=True)
    return r * (2.0 - x * r)


def dot_lanes(a, b):
    return lax.dot_general(a, b, (((1,), (1,)), ((), ())), preferred_element_type=F32)


def unpacked_centroids(sums):
    lane = lax.broadcasted_iota(jnp.int32, (8, 128), 1)
    row = lax.broadcasted_iota(jnp.int32, (8, 128), 0)
    denom = jnp.broadcast_to(sums[8:9, :], (8, 128))
    parts = []
    for g in range(4):
        d = jnp.sum(jnp.where(lane == row + 8 * g, denom, 0.0), axis=1, keepdims=True)
        parts.append(sums[0:8, 32 * g:32 * g + 32] / d)
    return jnp.concatenate(parts, axis=0)


def store_sums(part, numer, denom):
    part[0:8, :] = jnp.concatenate([numer[8 * g:8 * g + 8] for g in range(4)], axis=1)
    part[8:9, :] = jnp.concatenate([denom[0:1]] * 4, axis=1)


def prepare_kernel(attr, own, ends, rows):
    rows[...] = attr[...].astype(F32).reshape(F * COLS, 128)
    lane = lax.broadcasted_iota(jnp.int32, (1, 128), 1) // 4
    for half in range(2):
        acc = jnp.zeros((F, 128), F32)
        for j in range(32):
            c = half * 32 + j
            col = rows[pl.ds(c, F, stride=COLS), :]
            own[c] = col.astype(BF16)
            acc = jnp.where(lane == j, pltpu.roll(col, (4 * j + 2) % 128, 1), acc)
        ends[half] = acc.astype(BF16)


class Step:
    def __init__(self, cent, edge, band):
        c = unpacked_centroids(cent)
        self.cbm2 = (-2.0 * c.astype(BF16).astype(F32)).astype(BF16)
        self.csq1 = jnp.broadcast_to(jnp.sum(c * c, axis=1, keepdims=True) + 1.0, (F, 128))
        self.xlo, self.xhi, self.ylo, self.yhi, self.zlo, self.zhi = [edge[i] for i in range(6)]
        self.band = band
        self.lane = lax.broadcasted_iota(jnp.int32, (1, 128), 1)
        self.numer = jnp.zeros((F, F), F32)
        self.denom = jnp.zeros((8, F), F32)

    def inverse(self, a):
        af = a.astype(F32)
        sq = jnp.sum(af * af, axis=0, keepdims=True)
        cross = jnp.dot(self.cbm2, a, preferred_element_type=F32)
        return [
            recip(cross[:, s:s + 128] + self.csq1 + sq[:, s:s + 128])
            for s in range(0, a.shape[1], 128)
        ]

    def normalised(self, inv, mask):
        scale = recip(jnp.sum(inv, axis=0, keepdims=True))
        if mask is not None:
            scale = scale * mask
        return (inv * scale).astype(BF16)

    def front(self, X, column, keep):
        mx = self.xlo if X < 2 else (self.xhi if X >= W + 2 else None)
        rounded = []
        for Y in range(0, E, 2):
            my = self.ylo if Y < 2 else (self.yhi if Y >= W + 2 else None)
            m = mx if my is None else (my if mx is None else mx * my)
            pair = jnp.concatenate([column(X, Y), column(X, Y + 1)], axis=1)
            for i, inv in enumerate(self.inverse(pair)):
                if mx is None and my is None:
                    keep(Y + i - 2, inv)
                rounded.append(self.normalised(inv, m))
        z = jnp.dot(jnp.concatenate(rounded, axis=0), self.band[...], preferred_element_type=F32)
        cols = [z[F * Y:F * Y + F] for Y in range(E)]
        p = [cols[Y] + cols[Y + 1] for Y in range(E - 1)]
        return [p[y] + p[y + 2] + cols[y + 4] for y in range(W)]

    def halo(self, tiles, arrays, matrix):
        mz = jnp.where(self.lane % 4 < 2, self.zlo, self.zhi)
        rounded = []
        for (dx, dy, _), a in zip(tiles, arrays):
            m = mz
            if dx:
                m = m * (self.xlo if dx < 0 else self.xhi)
            if dy:
                m = m * (self.ylo if dy < 0 else self.yhi)
            rounded.append(self.normalised(self.inverse(a)[0], m))
        out = jnp.dot(jnp.concatenate(rounded, axis=1), matrix, preferred_element_type=F32)
        self.halves = out[:, :128], out[:, 128:]

    def halo_of(self, c):
        turned = pltpu.roll(self.halves[c // 32], (126 - 4 * (c % 32)) % 128, 1)
        return jnp.where((self.lane < 2) | (self.lane >= 126), turned, 0.0)

    def back(self, x, boxes, inv, own, memb=None):
        ws = []
        for y in range(W):
            prod = inv(y) * boxes[y]
            m = prod * recip(jnp.sum(prod, axis=0, keepdims=True))
            if memb is not None:
                memb[pl.ds(x * W + y, F, stride=COLS), :] = m
            ws.append((m * m).astype(BF16))
        w = jnp.concatenate(ws, axis=1)
        t = jnp.concatenate([own[x * W + y] for y in range(W)], axis=1)
        self.numer = self.numer + dot_lanes(w, t)
        self.denom = self.denom + dot_lanes(jnp.ones((8, W * 128), BF16), w)


def total(arrays):
    out = arrays[0]
    for a in arrays[1:]:
        out = out + a
    return out


def mid_column(own, ylo, yhi):
    def column(X, Y):
        x = X - 2
        if Y < 2:
            return ylo[x * 2 + Y]
        if Y >= W + 2:
            return yhi[x * 2 + Y - W - 2]
        return own[x * W + Y - 2]
    return column


def outer_column(xlo, xhi):
    def column(X, Y):
        ref, i = (xlo, X) if X < 2 else (xhi, X - W - 2)
        if Y < 2:
            return ref[16 + i * 2 + Y]
        if Y >= W + 2:
            return ref[20 + i * 2 + Y - W - 2]
        return ref[i * W + Y - 2]
    return column


def near_tiles(zown, ylo, yhi):
    return [zown[0], zown[1], ylo[16], ylo[17], yhi[16], yhi[17]]


def far_tiles(xlo, xhi):
    return [r[24 + i] for r in (xlo, xhi) for i in range(3)]


def inner_kernel(own, ylo, yhi, zown, cent, edge, band, near_hbm, box, kept, sums,
                 inv_s, win_s, near, sem):
    fetch = pltpu.make_async_copy(near_hbm, near, sem)
    fetch.start()
    step = Step(cent, edge, band)
    column = mid_column(own, ylo, yhi)
    for x in range(W):
        def keep(y, inv, x=x):
            if x in INNER:
                inv_s[(x - 2) * W + y] = inv
            else:
                kept[OUTER.index(x) * W + y] = inv
        for y, w in enumerate(step.front(x + 2, column, keep)):
            win_s[x * W + y] = w
    fetch.wait()
    step.halo(z_tiles()[0], near_tiles(zown, ylo, yhi), near[...])

    def mid_box(x, y):
        rows = range(max(x - 2, 0), min(x + 3, W))
        return total([win_s[r * W + y] for r in rows]) + step.halo_of(x * W + y)

    for x in INNER:
        step.back(x, [mid_box(x, y) for y in range(W)], lambda y: inv_s[(x - 2) * W + y], own)
    for i, x in enumerate(OUTER):
        for y in range(W):
            box[i * W + y] = mid_box(x, y)
    sums[0:F, :] = step.numer
    sums[F:F + 8, :] = step.denom


def outer_kernel(own, xlo, xhi, cent, edge, band, far_hbm, box, kept, sums, part,
                 win_s, far, sem):
    fetch = pltpu.make_async_copy(far_hbm, far, sem)
    fetch.start()
    step = Step(cent, edge, band)
    column = outer_column(xlo, xhi)
    rows = (0, 1, W + 2, W + 3)
    for i, X in enumerate(rows):
        for y, w in enumerate(step.front(X, column, None)):
            win_s[i * W + y] = w
    fetch.wait()
    step.halo(z_tiles()[1], far_tiles(xlo, xhi), far[...])
    for i, x in enumerate(OUTER):
        near = [n for n, X in enumerate(rows) if x <= X <= x + 4]
        boxes = [
            total([box[i * W + y]] + [win_s[n * W + y] for n in near]) + step.halo_of(x * W + y)
            for y in range(W)
        ]
        step.back(x, boxes, lambda y: kept[i * W + y], own)
    store_sums(part, step.numer + sums[0:F, :], step.denom + sums[F:F + 8, :])


def whole_kernel(own, ylo, yhi, xlo, xhi, zown, cent, edge, band, near_hbm, far_hbm, memb, part,
                 inv_s, win_s, matrix, sem):
    half = matrix.shape[0] // 2
    fetch = [
        pltpu.make_async_copy(near_hbm, matrix.at[0:half], sem.at[0]),
        pltpu.make_async_copy(far_hbm, matrix.at[half:2 * half], sem.at[1]),
    ]
    for f in fetch:
        f.start()
    step = Step(cent, edge, band)
    mid, outer = mid_column(own, ylo, yhi), outer_column(xlo, xhi)
    for X in range(E):
        def keep(y, inv, X=X):
            inv_s[(X - 2) * W + y] = inv
        for y, w in enumerate(step.front(X, mid if 2 <= X < W + 2 else outer, keep)):
            win_s[X * W + y] = w
    for f in fetch:
        f.wait()
    near, far = z_tiles()
    step.halo(near + far, near_tiles(zown, ylo, yhi) + far_tiles(xlo, xhi), matrix[...])
    for x in range(W):
        boxes = [
            total([win_s[X * W + y] for X in range(x, x + 5)]) + step.halo_of(x * W + y)
            for y in range(W)
        ]
        step.back(x, boxes, lambda y: inv_s[x * W + y], own, memb)
    store_sums(part, step.numer, step.denom)


VMEM = pl.BlockSpec(memory_space=pltpu.VMEM)
SMEM = pl.BlockSpec(memory_space=pltpu.SMEM)
ANY = pl.BlockSpec(memory_space=pl.ANY)


def call(kernel, out_shape, in_specs, scratch_shapes, flops, moved, args):
    return pl.pallas_call(
        kernel,
        out_shape=tuple(jax.ShapeDtypeStruct(s, t) for s, t in out_shape),
        in_specs=in_specs,
        out_specs=(VMEM,) * len(out_shape),
        scratch_shapes=scratch_shapes,
        compiler_params=pltpu.CompilerParams(vmem_limit_bytes=24 << 20),
        cost_estimate=pl.CostEstimate(flops=flops, bytes_accessed=moved, transcendentals=0),
    )(*args)


def columns(n, dtype=F32):
    return (n, F, 128), dtype


def prepare(attributes):
    return call(
        prepare_kernel, [columns(COLS, BF16), columns(2, BF16)], [VMEM],
        [pltpu.VMEM((F * COLS, 128), F32)], 10 ** 6, 1 << 20, (attributes,))


def inner_part(own, ylo, yhi, zown, cent, edge, band, near):
    return call(
        inner_kernel, [columns(4 * W), columns(4 * W), ((F + 8, F), F32)],
        [VMEM] * 5 + [SMEM, VMEM, ANY],
        [pltpu.VMEM(*columns(4 * W)), pltpu.VMEM(*columns(COLS)),
         pltpu.VMEM(near.shape, BF16), pltpu.SemaphoreType.DMA],
        5 * 10 ** 8, 3 << 20, (own, ylo, yhi, zown, cent, edge, band, near))


def outer_part(own, xlo, xhi, cent, edge, band, far, box, kept, sums):
    return call(
        outer_kernel, [((9, 128), F32)],
        [VMEM] * 4 + [SMEM, VMEM, ANY, VMEM, VMEM, VMEM],
        [pltpu.VMEM(*columns(4 * W)), pltpu.VMEM(far.shape, BF16), pltpu.SemaphoreType.DMA],
        2 * 10 ** 8, 2 << 20, (own, xlo, xhi, cent, edge, band, far, box, kept, sums))[0]


def whole_update(own, ylo, yhi, xlo, xhi, zown, cent, edge, band, near, far):
    return call(
        whole_kernel, [((F * COLS, 128), F32), ((9, 128), F32)],
        [VMEM] * 7 + [SMEM, VMEM, ANY, ANY],
        [pltpu.VMEM(*columns(COLS)), pltpu.VMEM(*columns(E * W)),
         pltpu.VMEM((2 * near.shape[0], near.shape[1]), BF16), pltpu.SemaphoreType.DMA((2,))],
        8 * 10 ** 8, 3 << 20, (own, ylo, yhi, xlo, xhi, zown, cent, edge, band, near, far))


def both_ways(up, down, axes, count):
    lo = lax.ppermute(up, axes, [(i, (i + 1) % count) for i in range(count)])
    hi = lax.ppermute(down, axes, [((i + 1) % count, i) for i in range(count)])
    return lo, hi


def gather_sum(part, axes, count):
    every = lax.all_to_all(jnp.broadcast_to(part[None], (count,) + part.shape), axes, 0, 0)
    return jnp.sum(every, axis=0)


def total_sums(part):
    part = part.reshape(9, 1, 128)
    part = part + lax.ppermute(part, "core", [(0, 1), (1, 0)])
    part = gather_sum(part, ("gz",), 8)
    return gather_sum(part, ("cx", "gy"), 16).reshape(9, 128)


def edges():
    gx, gy, gz = lax.axis_index(XS), lax.axis_index("gy"), lax.axis_index("gz")
    return jnp.stack([gx > 0, gx < 7, gy > 0, gy < 3, gz > 0, gz < 7]).astype(F32)


def per_device(attributes, start_centroids):
    edge = edges()
    band = jnp.asarray(band_matrix(), BF16)
    near, far = [jnp.asarray(halo_matrix(t), BF16) for t in z_tiles()]
    packed = start_centroids.reshape(4, 8, F).transpose(1, 0, 2).reshape(8, 128)
    cent = jnp.concatenate([packed, jnp.ones((1, 128), F32)])

    own, ends = prepare(attributes)
    zlo, zhi = both_ways(ends, ends, "gz", 8)
    lane = lax.broadcasted_iota(jnp.int32, ends.shape, 2)
    zown = jnp.where(lane % 4 < 2, zlo, zhi)

    grid = own.reshape(W, W, F, 128)

    def y_slice(y):
        return jnp.concatenate([grid[:, y:y + 2].reshape(2 * W, F, 128), zown])

    ylo, yhi = both_ways(y_slice(W - 2), y_slice(0), "gy", 4)

    def x_slice(x, half):
        return jnp.concatenate(
            [own[x * W:x * W + 2 * W], ylo[2 * x:2 * x + 4], yhi[2 * x:2 * x + 4],
             zown[half:half + 1], ylo[16 + half:17 + half], yhi[16 + half:17 + half]])

    xlo, xhi = both_ways(x_slice(W - 2, 1), x_slice(0, 0), XS, 8)

    box, kept, sums = inner_part(own, ylo, yhi, zown, cent, edge, band, near)
    part = outer_part(own, xlo, xhi, cent, edge, band, far, box, kept, sums)
    cent = total_sums(part)
    memb, part = whole_update(own, ylo, yhi, xlo, xhi, zown, cent, edge, band, near, far)
    cent = total_sums(part)
    numer = cent[:8].reshape(8, 4, F).transpose(1, 0, 2).reshape(F, F)
    return numer / cent[8, :F][:, None], memb.reshape(F, W, W, 128)


def solution(mesh):
    split = Mesh(np.asarray(mesh.devices).reshape(4, 2, 4, 8), ("cx", "core", "gy", "gz"))
    return jax.shard_map(
        per_device,
        mesh=split,
        in_specs=(P(None, XS, "gy", "gz"), P()),
        out_specs=(P(), P(None, XS, "gy", "gz")),
        check_vma=False,
    )
```

```python
import jax
import jax.numpy as jnp
import numpy as np
from jax import lax
from jax.experimental import pallas as pl
from jax.experimental.pallas import tpu as pltpu
from jax.sharding import Mesh, PartitionSpec as P

F = 32
W = 8
E = W + 4
COLS = W * W
BF16 = jnp.bfloat16
F32 = jnp.float32
XS = ("cx", "core")
OUTER = (0, 1, W - 2, W - 1)
INNER = tuple(range(2, W - 2))


def z_tiles():
    near = [(0, dy, half) for dy in (0, -1, 1) for half in (0, 1)]
    far = [(dx, dy, half) for dx, half in ((-1, 1), (1, 0)) for dy in (0, -1, 1)]
    return near, far


def halo_matrix(tiles):
    src = []
    for dx, dy, half in tiles:
        for c in range(half * 32, half * 32 + 32):
            for t in range(4):
                src.append((dx * W + c // W, dy * W + c % W, (-2, -1, 128, 129)[t]))
    dst = [(c // W, c % W, (126, 127, 0, 1)[t]) for c in range(COLS) for t in range(4)]
    gap = np.abs(np.array(src)[:, None, :] - np.array(dst)[None, :, :])
    return (gap <= 2).all(-1).astype(np.float32)


def band_matrix():
    z = np.arange(128)
    return (np.abs(z[:, None] - z[None, :]) <= 2).astype(np.float32)


def recip(x):
    r = pl.reciprocal(x, approx=True)
    return r * (2.0 - x * r)


def dot_lanes(a, b):
    return lax.dot_general(a, b, (((1,), (1,)), ((), ())), preferred_element_type=F32)


def unpacked_centroids(sums):
    lane = lax.broadcasted_iota(jnp.int32, (8, 128), 1)
    row = lax.broadcasted_iota(jnp.int32, (8, 128), 0)
    denom = jnp.broadcast_to(sums[8:9, :], (8, 128))
    parts = []
    for g in range(4):
        d = jnp.sum(jnp.where(lane == row + 8 * g, denom, 0.0), axis=1, keepdims=True)
        parts.append(sums[0:8, 32 * g:32 * g + 32] / d)
    return jnp.concatenate(parts, axis=0)


def store_sums(part, numer, denom):
    part[0:8, :] = jnp.concatenate([numer[8 * g:8 * g + 8] for g in range(4)], axis=1)
    part[8:9, :] = jnp.concatenate([denom[0:1]] * 4, axis=1)


def prepare_kernel(attr, own, ends, rows):
    rows[...] = attr[...].astype(F32).reshape(F * COLS, 128)
    lane = lax.broadcasted_iota(jnp.int32, (1, 128), 1) // 4
    for half in range(2):
        acc = jnp.zeros((F, 128), F32)
        for j in range(32):
            c = half * 32 + j
            col = rows[pl.ds(c, F, stride=COLS), :]
            own[c] = col.astype(BF16)
            acc = jnp.where(lane == j, pltpu.roll(col, (4 * j + 2) % 128, 1), acc)
        ends[half] = acc.astype(BF16)


def turned8(v):
    row = lax.broadcasted_iota(jnp.int32, (8, 128), 0)
    v = list(v)
    for s in (4, 2, 1):
        low = (row & s) == 0
        for i in range(8):
            if not i & s:
                a, b = v[i], v[i + s]
                v[i] = jnp.where(low, a, pltpu.roll(b, s, 0))
                v[i + s] = jnp.where(low, pltpu.roll(a, 8 - s, 0), b)
    return v


class Step:
    def __init__(self, cent, edge, band):
        c = unpacked_centroids(cent)
        self.cbm2 = (-2.0 * c.astype(BF16).astype(F32)).astype(BF16)
        self.csq1 = jnp.broadcast_to(jnp.sum(c * c, axis=1, keepdims=True) + 1.0, (F, 128))
        self.xlo, self.xhi, self.ylo, self.yhi, self.zlo, self.zhi = [edge[i] for i in range(6)]
        self.band = band
        self.lane = lax.broadcasted_iota(jnp.int32, (1, 128), 1)
        self.numer = jnp.zeros((F, F), F32)
        self.denom = jnp.zeros((8, F), F32)

    def inverse(self, a):
        af = a.astype(F32)
        sq = jnp.sum(af * af, axis=0, keepdims=True)
        cross = jnp.dot(self.cbm2, a, preferred_element_type=F32)
        return [
            recip(cross[:, s:s + 128] + self.csq1 + sq[:, s:s + 128])
            for s in range(0, a.shape[1], 128)
        ]

    def normalised(self, inv, mask):
        scale = recip(jnp.sum(inv, axis=0, keepdims=True))
        if mask is not None:
            scale = scale * mask
        return (inv * scale).astype(BF16)

    def front(self, X, column, keep):
        mx = self.xlo if X < 2 else (self.xhi if X >= W + 2 else None)
        rounded = []
        for Y in range(0, E, 2):
            my = self.ylo if Y < 2 else (self.yhi if Y >= W + 2 else None)
            m = mx if my is None else (my if mx is None else mx * my)
            pair = jnp.concatenate([column(X, Y), column(X, Y + 1)], axis=1)
            for i, inv in enumerate(self.inverse(pair)):
                if mx is None and my is None:
                    keep(Y + i - 2, inv)
                rounded.append(self.normalised(inv, m))
        z = jnp.dot(jnp.concatenate(rounded, axis=0), self.band[...], preferred_element_type=F32)
        cols = [z[F * Y:F * Y + F] for Y in range(E)]
        p = [cols[Y] + cols[Y + 1] for Y in range(E - 1)]
        return [p[y] + p[y + 2] + cols[y + 4] for y in range(W)]

    def halo(self, tiles, arrays, matrix):
        mz = jnp.where(self.lane % 4 < 2, self.zlo, self.zhi)
        rounded = []
        for (dx, dy, _), a in zip(tiles, arrays):
            m = mz
            if dx:
                m = m * (self.xlo if dx < 0 else self.xhi)
            if dy:
                m = m * (self.ylo if dy < 0 else self.yhi)
            rounded.append(self.normalised(self.inverse(a)[0], m))
        return jnp.dot(jnp.concatenate(rounded, axis=1), matrix[...], preferred_element_type=F32)

    def halo_of(self, windows, c):
        half = windows[:, c // 32 * 128:c // 32 * 128 + 128]
        turned = pltpu.roll(half, (126 - 4 * (c % 32)) % 128, 1)
        return jnp.where((self.lane < 2) | (self.lane >= 126), turned, 0.0)

    def back(self, x, boxes, inv, own, memb=None):
        ws, ms = [], []
        for y in range(W):
            prod = inv(y) * boxes[y]
            m = prod * recip(jnp.sum(prod, axis=0, keepdims=True))
            ms.append(m)
            ws.append((m * m).astype(BF16))
        if memb is not None:
            for g in range(4):
                for k, rows in enumerate(turned8([m[8 * g:8 * g + 8] for m in ms])):
                    memb[8 * g + k, x] = rows
        w = jnp.concatenate(ws, axis=1)
        t = jnp.concatenate([own[x * W + y] for y in range(W)], axis=1)
        self.numer = self.numer + dot_lanes(w, t)
        self.denom = self.denom + dot_lanes(jnp.ones((8, W * 128), BF16), w)


def total(arrays):
    out = arrays[0]
    for a in arrays[1:]:
        out = out + a
    return out


def mid_column(own, ylo, yhi):
    def column(X, Y):
        x = X - 2
        if Y < 2:
            return ylo[x * 2 + Y]
        if Y >= W + 2:
            return yhi[x * 2 + Y - W - 2]
        return own[x * W + Y - 2]
    return column


def outer_column(xlo, xhi):
    def column(X, Y):
        ref, i = (xlo, X) if X < 2 else (xhi, X - W - 2)
        if Y < 2:
            return ref[16 + i * 2 + Y]
        if Y >= W + 2:
            return ref[20 + i * 2 + Y - W - 2]
        return ref[i * W + Y - 2]
    return column


def near_tiles(zown, ylo, yhi):
    return [zown[0], zown[1], ylo[16], ylo[17], yhi[16], yhi[17]]


def far_tiles(xlo, xhi):
    return [r[24 + i] for r in (xlo, xhi) for i in range(3)]


def inner_kernel(own, ylo, yhi, zown, cent, edge, band, near, box, kept, sums, inv_s, win_s):
    step = Step(cent, edge, band)
    column = mid_column(own, ylo, yhi)
    windows = step.halo(z_tiles()[0], near_tiles(zown, ylo, yhi), near)
    for x in range(W):
        def keep(y, inv, x=x):
            if x in INNER:
                inv_s[(x - 2) * W + y] = inv
            else:
                kept[OUTER.index(x) * W + y] = inv
        for y, w in enumerate(step.front(x + 2, column, keep)):
            win_s[x * W + y] = w

    def mid_box(x, y):
        rows = range(max(x - 2, 0), min(x + 3, W))
        return total([win_s[r * W + y] for r in rows]) + step.halo_of(windows, x * W + y)

    for x in INNER:
        step.back(x, [mid_box(x, y) for y in range(W)], lambda y: inv_s[(x - 2) * W + y], own)
    for i, x in enumerate(OUTER):
        for y in range(W):
            box[i * W + y] = mid_box(x, y)
    sums[0:F, :] = step.numer
    sums[F:F + 8, :] = step.denom


def outer_kernel(own, xlo, xhi, cent, edge, band, far, box, kept, sums, part, win_s):
    step = Step(cent, edge, band)
    column = outer_column(xlo, xhi)
    rows = (0, 1, W + 2, W + 3)
    windows = step.halo(z_tiles()[1], far_tiles(xlo, xhi), far)
    for i, X in enumerate(rows):
        for y, w in enumerate(step.front(X, column, None)):
            win_s[i * W + y] = w
    for i, x in enumerate(OUTER):
        near = [n for n, X in enumerate(rows) if x <= X <= x + 4]
        boxes = [
            total([box[i * W + y]] + [win_s[n * W + y] for n in near]) + step.halo_of(windows, x * W + y)
            for y in range(W)
        ]
        step.back(x, boxes, lambda y: kept[i * W + y], own)
    store_sums(part, step.numer + sums[0:F, :], step.denom + sums[F:F + 8, :])


def whole_kernel(own, ylo, yhi, xlo, xhi, zown, cent, edge, band, near, far, memb, part, inv_s, win_s):
    step = Step(cent, edge, band)
    mid, outer = mid_column(own, ylo, yhi), outer_column(xlo, xhi)
    windows = step.halo(z_tiles()[0], near_tiles(zown, ylo, yhi), near)
    windows = windows + step.halo(z_tiles()[1], far_tiles(xlo, xhi), far)
    for X in range(E):
        def keep(y, inv, X=X):
            inv_s[(X - 2) * W + y] = inv
        for y, w in enumerate(step.front(X, mid if 2 <= X < W + 2 else outer, keep)):
            win_s[X * W + y] = w
    for x in range(W):
        boxes = [
            total([win_s[X * W + y] for X in range(x, x + 5)]) + step.halo_of(windows, x * W + y)
            for y in range(W)
        ]
        step.back(x, boxes, lambda y: inv_s[x * W + y], own, memb)
    store_sums(part, step.numer, step.denom)


VMEM = pl.BlockSpec(memory_space=pltpu.VMEM)
SMEM = pl.BlockSpec(memory_space=pltpu.SMEM)


def call(kernel, out_shape, in_specs, scratch_shapes, flops, moved, args):
    return pl.pallas_call(
        kernel,
        out_shape=tuple(jax.ShapeDtypeStruct(s, t) for s, t in out_shape),
        in_specs=in_specs,
        out_specs=(VMEM,) * len(out_shape),
        scratch_shapes=scratch_shapes,
        compiler_params=pltpu.CompilerParams(vmem_limit_bytes=24 << 20),
        cost_estimate=pl.CostEstimate(flops=flops, bytes_accessed=moved, transcendentals=0),
    )(*args)


def columns(n, dtype=F32):
    return (n, F, 128), dtype


def prepare(attributes):
    return call(
        prepare_kernel, [columns(COLS, BF16), columns(2, BF16)], [VMEM],
        [pltpu.VMEM((F * COLS, 128), F32)], 10 ** 6, 1 << 20, (attributes,))


def inner_part(own, ylo, yhi, zown, cent, edge, band, near):
    return call(
        inner_kernel, [columns(4 * W), columns(4 * W), ((F + 8, F), F32)],
        [VMEM] * 5 + [SMEM, VMEM, VMEM],
        [pltpu.VMEM(*columns(4 * W)), pltpu.VMEM(*columns(COLS))],
        5 * 10 ** 8, 3 << 20, (own, ylo, yhi, zown, cent, edge, band, near))


def outer_part(own, xlo, xhi, cent, edge, band, far, box, kept, sums):
    return call(
        outer_kernel, [((9, 128), F32)],
        [VMEM] * 4 + [SMEM] + [VMEM] * 5,
        [pltpu.VMEM(*columns(4 * W))],
        2 * 10 ** 8, 2 << 20, (own, xlo, xhi, cent, edge, band, far, box, kept, sums))[0]


def whole_update(own, ylo, yhi, xlo, xhi, zown, cent, edge, band, near, far):
    return call(
        whole_kernel, [((F, W, W, 128), F32), ((9, 128), F32)],
        [VMEM] * 7 + [SMEM] + [VMEM] * 3,
        [pltpu.VMEM(*columns(COLS)), pltpu.VMEM(*columns(E * W))],
        8 * 10 ** 8, 3 << 20, (own, ylo, yhi, xlo, xhi, zown, cent, edge, band, near, far))


def both_ways(up, down, axes, count):
    lo = lax.ppermute(up, axes, [(i, (i + 1) % count) for i in range(count)])
    hi = lax.ppermute(down, axes, [((i + 1) % count, i) for i in range(count)])
    return lo, hi


def gather_sum(part, axes, count):
    every = lax.all_to_all(jnp.broadcast_to(part[None], (count,) + part.shape), axes, 0, 0)
    return jnp.sum(every, axis=0)


def total_sums(part):
    part = part.reshape(9, 1, 128)
    part = part + lax.ppermute(part, "core", [(0, 1), (1, 0)])
    part = gather_sum(part, ("gz",), 8)
    return gather_sum(part, ("cx", "gy"), 16).reshape(9, 128)


def edges():
    gx, gy, gz = lax.axis_index(XS), lax.axis_index("gy"), lax.axis_index("gz")
    return jnp.stack([gx > 0, gx < 7, gy > 0, gy < 3, gz > 0, gz < 7]).astype(F32)


def per_device(attributes, start_centroids):
    edge = edges()
    band = jnp.asarray(band_matrix(), BF16)
    near, far = [jnp.asarray(halo_matrix(t), BF16) for t in z_tiles()]
    packed = start_centroids.reshape(4, 8, F).transpose(1, 0, 2).reshape(8, 128)
    cent = jnp.concatenate([packed, jnp.ones((1, 128), F32)])

    own, ends = prepare(attributes)
    zlo, zhi = both_ways(ends, ends, "gz", 8)
    lane = lax.broadcasted_iota(jnp.int32, ends.shape, 2)
    zown = jnp.where(lane % 4 < 2, zlo, zhi)

    grid = own.reshape(W, W, F, 128)

    def y_slice(y):
        return jnp.concatenate([grid[:, y:y + 2].reshape(2 * W, F, 128), zown])

    ylo, yhi = both_ways(y_slice(W - 2), y_slice(0), "gy", 4)

    def x_slice(x, half):
        return jnp.concatenate(
            [own[x * W:x * W + 2 * W], ylo[2 * x:2 * x + 4], yhi[2 * x:2 * x + 4],
             zown[half:half + 1], ylo[16 + half:17 + half], yhi[16 + half:17 + half]])

    xlo, xhi = both_ways(x_slice(W - 2, 1), x_slice(0, 0), XS, 8)

    box, kept, sums = inner_part(own, ylo, yhi, zown, cent, edge, band, near)
    part = outer_part(own, xlo, xhi, cent, edge, band, far, box, kept, sums)
    cent = total_sums(part)
    memb, part = whole_update(own, ylo, yhi, xlo, xhi, zown, cent, edge, band, near, far)
    cent = total_sums(part)
    numer = cent[:8].reshape(8, 4, F).transpose(1, 0, 2).reshape(F, F)
    return numer / cent[8, :F][:, None], memb


def solution(mesh):
    split = Mesh(np.asarray(mesh.devices).reshape(4, 2, 4, 8), ("cx", "core", "gy", "gz"))
    return jax.shard_map(
        per_device,
        mesh=split,
        in_specs=(P(None, XS, "gy", "gz"), P()),
        out_specs=(P(), P(None, XS, "gy", "gz")),
        check_vma=False,
    )
```

```python
import jax
import jax.numpy as jnp
import numpy as np
from jax import lax
from jax.experimental import pallas as pl
from jax.experimental.pallas import tpu as pltpu
from jax.sharding import Mesh, PartitionSpec as P

F = 32
W = 8
E = W + 4
COLS = W * W
BF16 = jnp.bfloat16
F32 = jnp.float32
XS = ("cx", "core")
OUTER = (0, 1, W - 2, W - 1)
INNER = tuple(range(2, W - 2))


def z_tiles():
    near = [(0, dy, half) for dy in (0, -1, 1) for half in (0, 1)]
    far = [(dx, dy, half) for dx, half in ((-1, 1), (1, 0)) for dy in (0, -1, 1)]
    return near, far


def halo_matrix(tiles):
    src = []
    for dx, dy, half in tiles:
        for c in range(half * 32, half * 32 + 32):
            for t in range(4):
                src.append((dx * W + c // W, dy * W + c % W, (-2, -1, 128, 129)[t]))
    dst = [(c // W, c % W, (126, 127, 0, 1)[t]) for c in range(COLS) for t in range(4)]
    gap = np.abs(np.array(src)[:, None, :] - np.array(dst)[None, :, :])
    return (gap <= 2).all(-1).astype(np.float32)


def band_matrix():
    gap = lax.broadcasted_iota(jnp.int32, (128, 128), 0) - lax.broadcasted_iota(jnp.int32, (128, 128), 1)
    return jnp.where(jnp.abs(gap) <= 2, 1.0, 0.0).astype(BF16)


def recip(x):
    r = pl.reciprocal(x, approx=True)
    return r * (2.0 - x * r)


def dot_lanes(a, b):
    return lax.dot_general(a, b, (((1,), (1,)), ((), ())), preferred_element_type=F32)


def unpacked_centroids(sums):
    lane = lax.broadcasted_iota(jnp.int32, (8, 128), 1)
    row = lax.broadcasted_iota(jnp.int32, (8, 128), 0)
    denom = jnp.broadcast_to(sums[8:9, :], (8, 128))
    parts = []
    for g in range(4):
        d = jnp.sum(jnp.where(lane == row + 8 * g, denom, 0.0), axis=1, keepdims=True)
        parts.append(sums[0:8, 32 * g:32 * g + 32] / d)
    return jnp.concatenate(parts, axis=0)


def store_sums(part, numer, denom):
    part[0:8, :] = jnp.concatenate([numer[8 * g:8 * g + 8] for g in range(4)], axis=1)
    part[8:9, :] = jnp.concatenate([denom[0:1]] * 4, axis=1)


def prepare_kernel(attr, start, own, ends, cent, rows):
    cent[0:8, :] = jnp.concatenate([start[8 * g:8 * g + 8, :] for g in range(4)], axis=1)
    cent[8:9, :] = jnp.ones((1, 128), F32)
    rows[...] = attr[...].astype(F32).reshape(F * COLS, 128)
    lane = lax.broadcasted_iota(jnp.int32, (1, 128), 1) // 4
    for half in range(2):
        acc = jnp.zeros((F, 128), F32)
        for j in range(32):
            c = half * 32 + j
            col = rows[pl.ds(c, F, stride=COLS), :]
            own[c] = col.astype(BF16)
            acc = jnp.where(lane == j, pltpu.roll(col, (4 * j + 2) % 128, 1), acc)
        ends[half] = acc.astype(BF16)


def turned8(v):
    row = lax.broadcasted_iota(jnp.int32, (8, 128), 0)
    v = list(v)
    for s in (4, 2, 1):
        low = (row & s) == 0
        for i in range(8):
            if not i & s:
                a, b = v[i], v[i + s]
                v[i] = jnp.where(low, a, pltpu.roll(b, s, 0))
                v[i + s] = jnp.where(low, pltpu.roll(a, 8 - s, 0), b)
    return v


class Step:
    def __init__(self, cent, edge):
        c = unpacked_centroids(cent)
        self.cbm2 = (-2.0 * c.astype(BF16).astype(F32)).astype(BF16)
        self.csq1 = jnp.broadcast_to(jnp.sum(c * c, axis=1, keepdims=True) + 1.0, (F, 128))
        self.xlo, self.xhi, self.ylo, self.yhi, self.zlo, self.zhi = [edge[i] for i in range(6)]
        self.band = band_matrix()
        self.lane = lax.broadcasted_iota(jnp.int32, (1, 128), 1)
        self.numer = jnp.zeros((F, F), F32)
        self.denom = jnp.zeros((8, F), F32)

    def inverse(self, a):
        af = a.astype(F32)
        sq = jnp.sum(af * af, axis=0, keepdims=True)
        cross = jnp.dot(self.cbm2, a, preferred_element_type=F32)
        return [
            recip(cross[:, s:s + 128] + self.csq1 + sq[:, s:s + 128])
            for s in range(0, a.shape[1], 128)
        ]

    def normalised(self, inv, mask):
        scale = recip(jnp.sum(inv, axis=0, keepdims=True))
        if mask is not None:
            scale = scale * mask
        return (inv * scale).astype(BF16)

    def front(self, X, column, keep):
        mx = self.xlo if X < 2 else (self.xhi if X >= W + 2 else None)
        rounded = []
        for Y in range(0, E, 2):
            my = self.ylo if Y < 2 else (self.yhi if Y >= W + 2 else None)
            m = mx if my is None else (my if mx is None else mx * my)
            pair = jnp.concatenate([column(X, Y), column(X, Y + 1)], axis=1)
            for i, inv in enumerate(self.inverse(pair)):
                if mx is None and my is None:
                    keep(Y + i - 2, inv)
                rounded.append(self.normalised(inv, m))
        z = jnp.dot(jnp.concatenate(rounded, axis=0), self.band, preferred_element_type=F32)
        cols = [z[F * Y:F * Y + F] for Y in range(E)]
        p = [cols[Y] + cols[Y + 1] for Y in range(E - 1)]
        return [p[y] + p[y + 2] + cols[y + 4] for y in range(W)]

    def halo(self, tiles, arrays, matrix):
        mz = jnp.where(self.lane % 4 < 2, self.zlo, self.zhi)
        rounded = []
        for (dx, dy, _), a in zip(tiles, arrays):
            m = mz
            if dx:
                m = m * (self.xlo if dx < 0 else self.xhi)
            if dy:
                m = m * (self.ylo if dy < 0 else self.yhi)
            rounded.append(self.normalised(self.inverse(a)[0], m))
        return jnp.dot(jnp.concatenate(rounded, axis=1), matrix[...], preferred_element_type=F32)

    def halo_of(self, windows, c):
        half = windows[:, c // 32 * 128:c // 32 * 128 + 128]
        turned = pltpu.roll(half, (126 - 4 * (c % 32)) % 128, 1)
        return jnp.where((self.lane < 2) | (self.lane >= 126), turned, 0.0)

    def back(self, x, boxes, inv, own, memb=None):
        ws, ms = [], []
        for y in range(W):
            prod = inv(y) * boxes[y]
            m = prod * recip(jnp.sum(prod, axis=0, keepdims=True))
            ms.append(m)
            ws.append((m * m).astype(BF16))
        if memb is not None:
            for g in range(4):
                for k, rows in enumerate(turned8([m[8 * g:8 * g + 8] for m in ms])):
                    memb[8 * g + k, x] = rows
        w = jnp.concatenate(ws, axis=1)
        t = jnp.concatenate([own[x * W + y] for y in range(W)], axis=1)
        self.numer = self.numer + dot_lanes(w, t)
        self.denom = self.denom + dot_lanes(jnp.ones((8, W * 128), BF16), w)


def total(arrays):
    out = arrays[0]
    for a in arrays[1:]:
        out = out + a
    return out


def mid_column(own, ylo, yhi):
    def column(X, Y):
        x = X - 2
        if Y < 2:
            return ylo[x * 2 + Y]
        if Y >= W + 2:
            return yhi[x * 2 + Y - W - 2]
        return own[x * W + Y - 2]
    return column


def outer_column(xlo, xhi):
    def column(X, Y):
        ref, i = (xlo, X) if X < 2 else (xhi, X - W - 2)
        if Y < 2:
            return ref[16 + i * 2 + Y]
        if Y >= W + 2:
            return ref[20 + i * 2 + Y - W - 2]
        return ref[i * W + Y - 2]
    return column


def near_tiles(*arrays):
    return [a[half] for a in arrays for half in range(2)]


def far_tiles(xlo, xhi):
    return [r[24 + i] for r in (xlo, xhi) for i in range(3)]


def inner_kernel(own, ylo, yhi, zown, zylo, zyhi, cent, edge, near, box, kept, sums, inv_s, win_s):
    step = Step(cent, edge)
    column = mid_column(own, ylo, yhi)
    windows = step.halo(z_tiles()[0], near_tiles(zown, zylo, zyhi), near)
    for x in range(W):
        def keep(y, inv, x=x):
            if x in INNER:
                inv_s[(x - 2) * W + y] = inv
            else:
                kept[OUTER.index(x) * W + y] = inv
        for y, w in enumerate(step.front(x + 2, column, keep)):
            win_s[x * W + y] = w

    def mid_box(x, y):
        rows = range(max(x - 2, 0), min(x + 3, W))
        return total([win_s[r * W + y] for r in rows]) + step.halo_of(windows, x * W + y)

    for x in INNER:
        step.back(x, [mid_box(x, y) for y in range(W)], lambda y: inv_s[(x - 2) * W + y], own)
    for i, x in enumerate(OUTER):
        for y in range(W):
            box[i * W + y] = mid_box(x, y)
    sums[0:F, :] = step.numer
    sums[F:F + 8, :] = step.denom


def outer_kernel(own, xlo, xhi, cent, edge, far, box, kept, sums, part, win_s):
    step = Step(cent, edge)
    column = outer_column(xlo, xhi)
    rows = (0, 1, W + 2, W + 3)
    windows = step.halo(z_tiles()[1], far_tiles(xlo, xhi), far)
    for i, X in enumerate(rows):
        for y, w in enumerate(step.front(X, column, None)):
            win_s[i * W + y] = w
    for i, x in enumerate(OUTER):
        near = [n for n, X in enumerate(rows) if x <= X <= x + 4]
        boxes = [
            total([box[i * W + y]] + [win_s[n * W + y] for n in near]) + step.halo_of(windows, x * W + y)
            for y in range(W)
        ]
        step.back(x, boxes, lambda y: kept[i * W + y], own)
    store_sums(part, step.numer + sums[0:F, :], step.denom + sums[F:F + 8, :])


def whole_kernel(own, ylo, yhi, xlo, xhi, zown, zylo, zyhi, cent, edge, near, far, memb, part, inv_s, win_s):
    step = Step(cent, edge)
    mid, outer = mid_column(own, ylo, yhi), outer_column(xlo, xhi)
    windows = step.halo(z_tiles()[0], near_tiles(zown, zylo, zyhi), near)
    windows = windows + step.halo(z_tiles()[1], far_tiles(xlo, xhi), far)
    for X in range(E):
        def keep(y, inv, X=X):
            inv_s[(X - 2) * W + y] = inv
        for y, w in enumerate(step.front(X, mid if 2 <= X < W + 2 else outer, keep)):
            win_s[X * W + y] = w
    for x in range(W):
        boxes = [
            total([win_s[X * W + y] for X in range(x, x + 5)]) + step.halo_of(windows, x * W + y)
            for y in range(W)
        ]
        step.back(x, boxes, lambda y: inv_s[x * W + y], own, memb)
    store_sums(part, step.numer, step.denom)


VMEM = pl.BlockSpec(memory_space=pltpu.VMEM)
SMEM = pl.BlockSpec(memory_space=pltpu.SMEM)


def call(kernel, out_shape, in_specs, scratch_shapes, flops, moved, args):
    return pl.pallas_call(
        kernel,
        out_shape=tuple(jax.ShapeDtypeStruct(s, t) for s, t in out_shape),
        in_specs=in_specs,
        out_specs=(VMEM,) * len(out_shape),
        scratch_shapes=scratch_shapes,
        compiler_params=pltpu.CompilerParams(vmem_limit_bytes=24 << 20),
        cost_estimate=pl.CostEstimate(flops=flops, bytes_accessed=moved, transcendentals=0),
    )(*args)


def columns(n, dtype=F32):
    return (n, F, 128), dtype


def prepare(attributes, start):
    return call(
        prepare_kernel, [columns(COLS, BF16), columns(2, BF16), ((9, 128), F32)], [VMEM] * 2,
        [pltpu.VMEM((F * COLS, 128), F32)], 10 ** 6, 1 << 20, (attributes, start))


def inner_part(own, ylo, yhi, zown, zylo, zyhi, cent, edge, near):
    return call(
        inner_kernel, [columns(4 * W), columns(4 * W), ((F + 8, F), F32)],
        [VMEM] * 7 + [SMEM, VMEM],
        [pltpu.VMEM(*columns(4 * W)), pltpu.VMEM(*columns(COLS))],
        5 * 10 ** 8, 3 << 20, (own, ylo, yhi, zown, zylo, zyhi, cent, edge, near))


def outer_part(own, xlo, xhi, cent, edge, far, box, kept, sums):
    return call(
        outer_kernel, [((9, 128), F32)],
        [VMEM] * 4 + [SMEM] + [VMEM] * 4,
        [pltpu.VMEM(*columns(4 * W))],
        2 * 10 ** 8, 2 << 20, (own, xlo, xhi, cent, edge, far, box, kept, sums))[0]


def whole_update(own, ylo, yhi, xlo, xhi, zown, zylo, zyhi, cent, edge, near, far):
    return call(
        whole_kernel, [((F, W, W, 128), F32), ((9, 128), F32)],
        [VMEM] * 9 + [SMEM] + [VMEM] * 2,
        [pltpu.VMEM(*columns(COLS)), pltpu.VMEM(*columns(E * W))],
        8 * 10 ** 8, 3 << 20, (own, ylo, yhi, xlo, xhi, zown, zylo, zyhi, cent, edge, near, far))


def both_ways(up, down, axes, count):
    lo = lax.ppermute(up, axes, [(i, (i + 1) % count) for i in range(count)])
    hi = lax.ppermute(down, axes, [((i + 1) % count, i) for i in range(count)])
    return lo, hi


def gather_sum(part, axes, count):
    every = lax.all_to_all(jnp.broadcast_to(part[None], (count,) + part.shape), axes, 0, 0)
    return jnp.sum(every, axis=0)


def total_sums(part):
    part = gather_sum(part.reshape(9, 1, 128), ("core", "gz"), 16)
    return gather_sum(part, ("cx", "gy"), 16).reshape(9, 128)


def edges():
    gx, gy, gz = lax.axis_index(XS), lax.axis_index("gy"), lax.axis_index("gz")
    return jnp.stack([gx > 0, gx < 7, gy > 0, gy < 3, gz > 0, gz < 7]).astype(F32)


def per_device(attributes, start_centroids):
    edge = edges()
    near, far = [jnp.asarray(halo_matrix(t), BF16) for t in z_tiles()]
    own, ends, cent = prepare(attributes, start_centroids)
    zlo, zhi = both_ways(ends, ends, "gz", 8)
    lane = lax.broadcasted_iota(jnp.int32, ends.shape, 2)
    zown = jnp.where(lane % 4 < 2, zlo, zhi)

    grid = own.reshape(W, W, F, 128)
    ylo, yhi = both_ways(
        grid[:, W - 2:].reshape(2 * W, F, 128), grid[:, :2].reshape(2 * W, F, 128), "gy", 4)
    zylo, zyhi = both_ways(zown, zown, "gy", 4)

    def x_slice(x, half):
        return jnp.concatenate(
            [own[x * W:x * W + 2 * W], ylo[2 * x:2 * x + 4], yhi[2 * x:2 * x + 4],
             zown[half:half + 1], zylo[half:half + 1], zyhi[half:half + 1]])

    xlo, xhi = both_ways(x_slice(W - 2, 1), x_slice(0, 0), XS, 8)

    box, kept, sums = inner_part(own, ylo, yhi, zown, zylo, zyhi, cent, edge, near)
    part = outer_part(own, xlo, xhi, cent, edge, far, box, kept, sums)
    cent = total_sums(part)
    memb, part = whole_update(own, ylo, yhi, xlo, xhi, zown, zylo, zyhi, cent, edge, near, far)
    cent = total_sums(part)
    numer = cent[:8].reshape(8, 4, F).transpose(1, 0, 2).reshape(F, F)
    return numer / cent[8, :F][:, None], memb


def solution(mesh):
    split = Mesh(np.asarray(mesh.devices).reshape(4, 2, 4, 8), ("cx", "core", "gy", "gz"))
    return jax.shard_map(
        per_device,
        mesh=split,
        in_specs=(P(None, XS, "gy", "gz"), P()),
        out_specs=(P(), P(None, XS, "gy", "gz")),
        check_vma=False,
    )
```

```python
import jax
import jax.numpy as jnp
import numpy as np
from jax import lax
from jax.experimental import pallas as pl
from jax.experimental.pallas import tpu as pltpu
from jax.sharding import Mesh, PartitionSpec as P

F = 32
W = 8
E = W + 4
COLS = W * W
BF16 = jnp.bfloat16
F32 = jnp.float32
XS = ("cx", "core")
OUTER = (0, 1, W - 2, W - 1)
INNER = tuple(range(2, W - 2))
ROWS = (0, 1, W + 2, W + 3)


def tile_columns():
    def beyond(i):
        return i - W if i >= W // 2 else i + W

    own = [(c // W, c % W) for c in range(COLS)]
    ys = [(x, beyond(y)) for x, y in own]
    xs = [(beyond(j // W + (4 if j >= 16 else 0)), j % W) for j in range(32)]
    return own + ys + xs + [(x, beyond(y)) for x, y in xs]


def halo_matrix():
    src = [(x, y, z) for x, y in tile_columns() for z in (-2, -1, 128, 129)]
    dst = [(c // W, c % W, z) for c in range(COLS) for z in (126, 127, 0, 1)]
    gap = np.abs(np.array(src)[:, None, :] - np.array(dst)[None, :, :])
    return (gap <= 2).all(-1).astype(np.float32)


def band_matrix():
    gap = lax.broadcasted_iota(jnp.int32, (128, 128), 0) - lax.broadcasted_iota(jnp.int32, (128, 128), 1)
    return jnp.where(jnp.abs(gap) <= 2, 1.0, 0.0).astype(BF16)


def recip(x):
    r = pl.reciprocal(x, approx=True)
    return r * (2.0 - x * r)


def dot_lanes(a, b):
    return lax.dot_general(a, b, (((1,), (1,)), ((), ())), preferred_element_type=F32)


def unpacked_centroids(sums):
    lane = lax.broadcasted_iota(jnp.int32, (8, 128), 1)
    row = lax.broadcasted_iota(jnp.int32, (8, 128), 0)
    denom = jnp.broadcast_to(sums[8:9, :], (8, 128))
    parts = []
    for g in range(4):
        d = jnp.sum(jnp.where(lane == row + 8 * g, denom, 0.0), axis=1, keepdims=True)
        parts.append(sums[0:8, 32 * g:32 * g + 32] / d)
    return jnp.concatenate(parts, axis=0)


def store_sums(part, numer, denom):
    part[0:8, :] = jnp.concatenate([numer[8 * g:8 * g + 8] for g in range(4)], axis=1)
    part[8:9, :] = jnp.concatenate([denom[0:1]] * 4, axis=1)


def turned8(v):
    row = lax.broadcasted_iota(jnp.int32, (8, 128), 0)
    v = list(v)
    for s in (4, 2, 1):
        low = (row & s) == 0
        for i in range(8):
            if not i & s:
                a, b = v[i], v[i + s]
                v[i] = jnp.where(low, a, pltpu.roll(b, s, 0))
                v[i + s] = jnp.where(low, pltpu.roll(a, 8 - s, 0), b)
    return v


def prepare_kernel(attr_hbm, start_hbm, own, ends, cent, attr, start, sems):
    fetch = [
        pltpu.make_async_copy(attr_hbm.at[:, x:x + 4], attr.at[:, x:x + 4], sems.at[x // 4])
        for x in range(0, W, 4)
    ]
    fetch.append(pltpu.make_async_copy(start_hbm, start, sems.at[2]))
    for f in fetch:
        f.start()
    lane = lax.broadcasted_iota(jnp.int32, (1, 128), 1) // 4
    for half in range(2):
        acc = jnp.zeros((F, 128), F32)
        fetch[half].wait()
        for x in range(half * 4, half * 4 + 4):
            wide = [attr[a, x].astype(F32) for a in range(F)]
            groups = [turned8(wide[8 * g:8 * g + 8]) for g in range(4)]
            for y in range(W):
                c = x * W + y
                j = c % 32
                col = jnp.concatenate([groups[g][y] for g in range(4)], axis=0)
                own[c] = col.astype(BF16)
                acc = jnp.where(lane == j, pltpu.roll(col, (4 * j + 2) % 128, 1), acc)
        ends[half] = acc.astype(BF16)
    fetch[-1].wait()
    cent[0:8, :] = jnp.concatenate([start[8 * g:8 * g + 8, :] for g in range(4)], axis=1)
    cent[8:9, :] = jnp.ones((1, 128), F32)


class Step:
    def __init__(self, cent, edge):
        c = unpacked_centroids(cent)
        self.cbm2 = (-2.0 * c.astype(BF16).astype(F32)).astype(BF16)
        self.csq1 = jnp.broadcast_to(jnp.sum(c * c, axis=1, keepdims=True) + 1.0, (F, 128))
        self.xlo, self.xhi, self.ylo, self.yhi, self.zlo, self.zhi = [edge[i] for i in range(6)]
        self.band = band_matrix()
        self.lane = lax.broadcasted_iota(jnp.int32, (1, 128), 1)
        self.numer = jnp.zeros((F, F), F32)
        self.denom = jnp.zeros((8, F), F32)

    def inverse(self, a):
        af = a.astype(F32)
        sq = jnp.sum(af * af, axis=0, keepdims=True)
        cross = jnp.dot(self.cbm2, a, preferred_element_type=F32)
        return [
            recip(cross[:, s:s + 128] + self.csq1 + sq[:, s:s + 128])
            for s in range(0, a.shape[1], 128)
        ]

    def normalised(self, inv, mask):
        scale = recip(jnp.sum(inv, axis=0, keepdims=True))
        if mask is not None:
            scale = scale * mask
        return (inv * scale).astype(BF16)

    def front(self, X, column, keep):
        mx = self.xlo if X < 2 else (self.xhi if X >= W + 2 else None)
        rounded = []
        for Y in range(0, E, 2):
            my = self.ylo if Y < 2 else (self.yhi if Y >= W + 2 else None)
            m = mx if my is None else (my if mx is None else mx * my)
            pair = jnp.concatenate([column(X, Y), column(X, Y + 1)], axis=1)
            for i, inv in enumerate(self.inverse(pair)):
                if mx is None and my is None:
                    keep(Y + i - 2, inv)
                rounded.append(self.normalised(inv, m))
        z = jnp.dot(jnp.concatenate(rounded, axis=0), self.band, preferred_element_type=F32)
        cols = [z[F * Y:F * Y + F] for Y in range(E)]
        p = [cols[Y] + cols[Y + 1] for Y in range(E - 1)]
        return [p[y] + p[y + 2] + cols[y + 4] for y in range(W)]

    def halo(self, tiles, matrix, near):
        j = self.lane // 4
        mz = jnp.where(self.lane % 4 < 2, self.zlo, self.zhi)
        my = mz * jnp.where(j % W >= W // 2, self.ylo, self.yhi)
        mx = jnp.where(j >= 16, self.xlo, self.xhi)
        masks = [mz, mz, my, my] if near else [mz * mx, my * mx]
        rounded = []
        for i in range(0, len(tiles), 2):
            pair = jnp.concatenate([tiles[i], tiles[i + 1]], axis=1)
            for inv, m in zip(self.inverse(pair), masks[i:i + 2]):
                rounded.append(self.normalised(inv, m))
        return jnp.dot(jnp.concatenate(rounded, axis=1), matrix, preferred_element_type=F32)

    def near_halo(self, zown, zy, matrix):
        return self.halo([zown[0], zown[1], zy[0], zy[1]], matrix[0:4 * 128, :], True)

    def far_halo(self, xlo, xhi, matrix):
        tiles = [jnp.where(self.lane >= 64, xlo[2 * E + i].astype(F32), xhi[2 * E + i].astype(F32)).astype(BF16)
                 for i in range(2)]
        return self.halo(tiles, matrix[4 * 128:6 * 128, :], False)

    def halo_of(self, windows, c):
        half = windows[:, c // 32 * 128:c // 32 * 128 + 128]
        turned = pltpu.roll(half, (126 - 4 * (c % 32)) % 128, 1)
        return jnp.where((self.lane < 2) | (self.lane >= 126), turned, 0.0)

    def back(self, x, boxes, inv, own, memb=None):
        ws, ms = [], []
        for y in range(W):
            prod = inv(y) * boxes[y]
            m = prod * recip(jnp.sum(prod, axis=0, keepdims=True))
            ms.append(m)
            ws.append((m * m).astype(BF16))
        if memb is not None:
            for g in range(4):
                for k, rows in enumerate(turned8([m[8 * g:8 * g + 8] for m in ms])):
                    memb[8 * g + k, x] = rows
        w = jnp.concatenate(ws, axis=1)
        t = jnp.concatenate([own[x * W + y] for y in range(W)], axis=1)
        self.numer = self.numer + dot_lanes(w, t)
        self.denom = self.denom + dot_lanes(jnp.ones((8, W * 128), BF16), w)


def total(arrays):
    out = arrays[0]
    for a in arrays[1:]:
        out = out + a
    return out


def mid_column(own, ylo, yhi):
    def column(X, Y):
        x = X - 2
        if Y < 2:
            return ylo[x * 2 + Y]
        if Y >= W + 2:
            return yhi[x * 2 + Y - W - 2]
        return own[x * W + Y - 2]
    return column


def outer_column(xlo, xhi):
    def column(X, Y):
        ref, i = (xlo, X) if X < 2 else (xhi, X - W - 2)
        if Y < 2:
            return ref[16 + i * 2 + Y]
        if Y >= W + 2:
            return ref[20 + i * 2 + Y - W - 2]
        return ref[i * W + Y - 2]
    return column


def inner_kernel(own, ylo, yhi, zown, zy, matrix, cent, edge, box, kept, sums, inv_s, win_s):
    step = Step(cent, edge)
    column = mid_column(own, ylo, yhi)
    windows = step.near_halo(zown, zy, matrix)
    for x in range(W):
        def keep(y, inv, x=x):
            if x in INNER:
                inv_s[(x - 2) * W + y] = inv
            else:
                kept[OUTER.index(x) * W + y] = inv
        for y, w in enumerate(step.front(x + 2, column, keep)):
            win_s[x * W + y] = w

    def mid_box(x, y):
        rows = range(max(x - 2, 0), min(x + 3, W))
        return total([win_s[r * W + y] for r in rows]) + step.halo_of(windows, x * W + y)

    for x in INNER:
        step.back(x, [mid_box(x, y) for y in range(W)], lambda y: inv_s[(x - 2) * W + y], own)
    for i, x in enumerate(OUTER):
        for y in range(W):
            box[i * W + y] = mid_box(x, y)
    sums[0:F, :] = step.numer
    sums[F:F + 8, :] = step.denom


def outer_kernel(own, xlo, xhi, matrix, cent, edge, box, kept, sums, part, win_s):
    step = Step(cent, edge)
    column = outer_column(xlo, xhi)
    windows = step.far_halo(xlo, xhi, matrix)
    for i, X in enumerate(ROWS):
        for y, w in enumerate(step.front(X, column, None)):
            win_s[i * W + y] = w
    for i, x in enumerate(OUTER):
        near = [n for n, X in enumerate(ROWS) if x <= X <= x + 4]
        boxes = [
            total([box[i * W + y]] + [win_s[n * W + y] for n in near])
            + step.halo_of(windows, x * W + y)
            for y in range(W)
        ]
        step.back(x, boxes, lambda y: kept[i * W + y], own)
    store_sums(part, step.numer + sums[0:F, :], step.denom + sums[F:F + 8, :])


def whole_kernel(own, ylo, yhi, xlo, xhi, zown, zy, matrix, cent, edge, memb, part, inv_s, win_s):
    step = Step(cent, edge)
    mid, outer = mid_column(own, ylo, yhi), outer_column(xlo, xhi)
    windows = step.near_halo(zown, zy, matrix) + step.far_halo(xlo, xhi, matrix)
    for X in range(E):
        def keep(y, inv, X=X):
            inv_s[(X - 2) * W + y] = inv
        for y, w in enumerate(step.front(X, mid if 2 <= X < W + 2 else outer, keep)):
            win_s[X * W + y] = w
    for x in range(W):
        boxes = [
            total([win_s[X * W + y] for X in range(x, x + 5)]) + step.halo_of(windows, x * W + y)
            for y in range(W)
        ]
        step.back(x, boxes, lambda y: inv_s[x * W + y], own, memb)
    store_sums(part, step.numer, step.denom)


VMEM = pl.BlockSpec(memory_space=pltpu.VMEM)
ANY = pl.BlockSpec(memory_space=pl.ANY)
SMEM = pl.BlockSpec(memory_space=pltpu.SMEM)


def call(kernel, out_shape, in_specs, scratch_shapes, flops, moved, args):
    return pl.pallas_call(
        kernel,
        out_shape=tuple(jax.ShapeDtypeStruct(s, t) for s, t in out_shape),
        in_specs=in_specs,
        out_specs=(VMEM,) * len(out_shape),
        scratch_shapes=scratch_shapes,
        compiler_params=pltpu.CompilerParams(vmem_limit_bytes=24 << 20),
        cost_estimate=pl.CostEstimate(flops=flops, bytes_accessed=moved, transcendentals=0),
    )(*args)


def columns(n, dtype=F32):
    return (n, F, 128), dtype


def prepare(attributes, start):
    return call(
        prepare_kernel, [columns(COLS, BF16), columns(2, BF16), ((9, 128), F32)], [ANY] * 2,
        [pltpu.VMEM(attributes.shape, BF16), pltpu.VMEM(start.shape, F32),
         pltpu.SemaphoreType.DMA((3,))],
        10 ** 6, 1 << 20,
        [pltpu.with_memory_space_constraint(a, pltpu.HBM) for a in (attributes, start)])


def inner_part(own, ylo, yhi, zown, zy, matrix, cent, edge):
    return call(
        inner_kernel, [columns(4 * W), columns(4 * W), ((F + 8, F), F32)], [VMEM] * 7 + [SMEM],
        [pltpu.VMEM(*columns(4 * W)), pltpu.VMEM(*columns(COLS))],
        5 * 10 ** 8, 3 << 20, (own, ylo, yhi, zown, zy, matrix, cent, edge))


def outer_part(own, xlo, xhi, matrix, cent, edge, box, kept, sums):
    return call(
        outer_kernel, [((9, 128), F32)], [VMEM] * 5 + [SMEM] + [VMEM] * 3,
        [pltpu.VMEM(*columns(4 * W))],
        2 * 10 ** 8, 2 << 20, (own, xlo, xhi, matrix, cent, edge, box, kept, sums))[0]


def whole_update(own, ylo, yhi, xlo, xhi, zown, zy, matrix, cent, edge):
    return call(
        whole_kernel, [((F, W, W, 128), F32), ((9, 128), F32)], [VMEM] * 9 + [SMEM],
        [pltpu.VMEM(*columns(COLS)), pltpu.VMEM(*columns(E * W))],
        8 * 10 ** 8, 3 << 20, (own, ylo, yhi, xlo, xhi, zown, zy, matrix, cent, edge))


def both_ways(up, down, axes, count):
    lo = lax.ppermute(up, axes, [(i, (i + 1) % count) for i in range(count)])
    hi = lax.ppermute(down, axes, [((i + 1) % count, i) for i in range(count)])
    return lo, hi


def gather_sum(part, axes, count):
    every = lax.all_to_all(jnp.broadcast_to(part[None], (count,) + part.shape), axes, 0, 0)
    return jnp.sum(every, axis=0)


def total_sums(part):
    part = gather_sum(part.reshape(9, 1, 128), ("core", "gz"), 16)
    return gather_sum(part, ("cx", "gy"), 16).reshape(9, 128)


def edges():
    gx, gy, gz = lax.axis_index(XS), lax.axis_index("gy"), lax.axis_index("gz")
    return jnp.stack([gx > 0, gx < 7, gy > 0, gy < 3, gz > 0, gz < 7]).astype(F32)


def per_device(attributes, start_centroids):
    edge = edges()
    matrix = jnp.asarray(halo_matrix(), BF16)
    lane = lax.broadcasted_iota(jnp.int32, (1, 1, 128), 2)
    own, ends, cent = prepare(attributes, start_centroids)
    grid = own.reshape(W, W, F, 128)
    ylo, yhi = both_ways(
        grid[:, W - 2:].reshape(2 * W, F, 128), grid[:, :2].reshape(2 * W, F, 128), "gy", 4)
    zlo, zhi = both_ways(ends, ends, "gz", 8)
    zown = jnp.where(lane % 4 < 2, zlo, zhi)
    zylo, zyhi = both_ways(zown, zown, "gy", 4)
    zy = jnp.where(lane // 4 % W >= W // 2, zylo, zyhi)

    def x_slice(x, half):
        return jnp.concatenate(
            [own[x * W:x * W + 2 * W], ylo[2 * x:2 * x + 4], yhi[2 * x:2 * x + 4],
             zown[half:half + 1], zy[half:half + 1]])

    xlo, xhi = both_ways(x_slice(W - 2, 1), x_slice(0, 0), XS, 8)

    box, kept, sums = inner_part(own, ylo, yhi, zown, zy, matrix, cent, edge)
    part = outer_part(own, xlo, xhi, matrix, cent, edge, box, kept, sums)
    cent = total_sums(part)
    memb, part = whole_update(own, ylo, yhi, xlo, xhi, zown, zy, matrix, cent, edge)
    cent = total_sums(part)
    numer = cent[:8].reshape(8, 4, F).transpose(1, 0, 2).reshape(F, F)
    return numer / cent[8, :F][:, None], memb


def solution(mesh):
    split = Mesh(np.asarray(mesh.devices).reshape(4, 2, 4, 8), ("cx", "core", "gy", "gz"))
    return jax.shard_map(
        per_device,
        mesh=split,
        in_specs=(P(None, XS, "gy", "gz"), P()),
        out_specs=(P(), P(None, XS, "gy", "gz")),
        check_vma=False,
    )
```

```python
import jax
import jax.numpy as jnp
import numpy as np
from jax import lax
from jax.experimental import pallas as pl
from jax.experimental.pallas import tpu as pltpu
from jax.sharding import Mesh, PartitionSpec as P

F = 32
W = 8
E = W + 4
COLS = W * W
BF16 = jnp.bfloat16
F32 = jnp.float32
XS = ("cx", "core")
OUTER = (0, 1, W - 2, W - 1)
INNER = tuple(range(2, W - 2))
ROWS = (0, 1, W + 2, W + 3)


def tile_columns():
    def beyond(i):
        return i - W if i >= W // 2 else i + W

    own = [(c // W, c % W) for c in range(COLS)]
    ys = [(x, beyond(y)) for x, y in own]
    xs = [(beyond(j // W + (4 if j >= 16 else 0)), j % W) for j in range(32)]
    return own + ys + xs + [(x, beyond(y)) for x, y in xs]


def halo_matrix():
    src = [(x, y, z) for x, y in tile_columns() for z in (-2, -1, 128, 129)]
    dst = [(c // W, c % W, z) for c in range(COLS) for z in (126, 127, 0, 1)]
    gap = np.abs(np.array(src)[:, None, :] - np.array(dst)[None, :, :])
    return (gap <= 2).all(-1).astype(np.float32)


def band_matrix():
    gap = lax.broadcasted_iota(jnp.int32, (128, 128), 0) - lax.broadcasted_iota(jnp.int32, (128, 128), 1)
    return jnp.where(jnp.abs(gap) <= 2, 1.0, 0.0).astype(BF16)


def recip(x):
    r = pl.reciprocal(x, approx=True)
    return r * (2.0 - x * r)


def dot_lanes(a, b):
    return lax.dot_general(a, b, (((1,), (1,)), ((), ())), preferred_element_type=F32)


def unpacked_centroids(sums):
    lane = lax.broadcasted_iota(jnp.int32, (8, 128), 1)
    row = lax.broadcasted_iota(jnp.int32, (8, 128), 0)
    denom = jnp.broadcast_to(sums[8:9, :], (8, 128))
    parts = []
    for g in range(4):
        d = jnp.sum(jnp.where(lane == row + 8 * g, denom, 0.0), axis=1, keepdims=True)
        parts.append(sums[0:8, 32 * g:32 * g + 32] / d)
    return jnp.concatenate(parts, axis=0)


def store_sums(part, numer, denom):
    part[0:8, :] = jnp.concatenate([numer[8 * g:8 * g + 8] for g in range(4)], axis=1)
    part[8:9, :] = jnp.concatenate([denom[0:1]] * 4, axis=1)


def turned8(v):
    row = lax.broadcasted_iota(jnp.int32, (8, 128), 0)
    v = list(v)
    for s in (4, 2, 1):
        low = (row & s) == 0
        for i in range(8):
            if not i & s:
                a, b = v[i], v[i + s]
                v[i] = jnp.where(low, a, pltpu.roll(b, s, 0))
                v[i + s] = jnp.where(low, pltpu.roll(a, 8 - s, 0), b)
    return v


def prepare_kernel(attr_hbm, start_hbm, own, ends, cent, attr, start, sems):
    fetch = [
        pltpu.make_async_copy(attr_hbm.at[:, x:x + 4], attr.at[:, x:x + 4], sems.at[x // 4])
        for x in range(0, W, 4)
    ]
    fetch.append(pltpu.make_async_copy(start_hbm, start, sems.at[2]))
    for f in fetch:
        f.start()
    lane = lax.broadcasted_iota(jnp.int32, (1, 128), 1) // 4
    for half in range(2):
        acc = jnp.zeros((F, 128), F32)
        fetch[half].wait()
        for x in range(half * 4, half * 4 + 4):
            wide = [attr[a, x].astype(F32) for a in range(F)]
            groups = [turned8(wide[8 * g:8 * g + 8]) for g in range(4)]
            for y in range(W):
                c = x * W + y
                j = c % 32
                col = jnp.concatenate([groups[g][y] for g in range(4)], axis=0)
                own[c] = col.astype(BF16)
                acc = jnp.where(lane == j, pltpu.roll(col, (4 * j + 2) % 128, 1), acc)
        ends[half] = acc.astype(BF16)
    fetch[-1].wait()
    cent[0:8, :] = jnp.concatenate([start[8 * g:8 * g + 8, :] for g in range(4)], axis=1)
    cent[8:9, :] = jnp.ones((1, 128), F32)


class Step:
    def __init__(self, cent, edge):
        c = unpacked_centroids(cent)
        self.cbm2 = (-2.0 * c.astype(BF16).astype(F32)).astype(BF16)
        self.csq1 = jnp.broadcast_to(jnp.sum(c * c, axis=1, keepdims=True) + 1.0, (F, 128))
        self.xlo, self.xhi, self.ylo, self.yhi, self.zlo, self.zhi = [edge[i:i + 1, :] for i in range(6)]
        self.band = band_matrix()
        self.lane = lax.broadcasted_iota(jnp.int32, (1, 128), 1)
        self.numer = jnp.zeros((F, F), F32)
        self.denom = jnp.zeros((8, F), F32)

    def inverse(self, a):
        af = a.astype(F32)
        sq = jnp.sum(af * af, axis=0, keepdims=True)
        cross = jnp.dot(self.cbm2, a, preferred_element_type=F32)
        return [
            recip(cross[:, s:s + 128] + self.csq1 + sq[:, s:s + 128])
            for s in range(0, a.shape[1], 128)
        ]

    def normalised(self, inv, mask):
        scale = recip(jnp.sum(inv, axis=0, keepdims=True))
        if mask is not None:
            scale = scale * mask
        return (inv * scale).astype(BF16)

    def front(self, X, column, keep):
        mx = self.xlo if X < 2 else (self.xhi if X >= W + 2 else None)
        rounded = []
        for Y in range(0, E, 2):
            my = self.ylo if Y < 2 else (self.yhi if Y >= W + 2 else None)
            m = mx if my is None else (my if mx is None else mx * my)
            pair = jnp.concatenate([column(X, Y), column(X, Y + 1)], axis=1)
            for i, inv in enumerate(self.inverse(pair)):
                if mx is None and my is None:
                    keep(Y + i - 2, inv)
                rounded.append(self.normalised(inv, m))
        z = jnp.dot(jnp.concatenate(rounded, axis=0), self.band, preferred_element_type=F32)
        cols = [z[F * Y:F * Y + F] for Y in range(E)]
        p = [cols[Y] + cols[Y + 1] for Y in range(E - 1)]
        return [p[y] + p[y + 2] + cols[y + 4] for y in range(W)]

    def halo(self, tiles, matrix, near):
        j = self.lane // 4
        mz = jnp.where(self.lane % 4 < 2, self.zlo, self.zhi)
        my = mz * jnp.where(j % W >= W // 2, self.ylo, self.yhi)
        mx = jnp.where(j >= 16, self.xlo, self.xhi)
        masks = [mz, mz, my, my] if near else [mz * mx, my * mx]
        rounded = []
        for i in range(0, len(tiles), 2):
            pair = jnp.concatenate([tiles[i], tiles[i + 1]], axis=1)
            for inv, m in zip(self.inverse(pair), masks[i:i + 2]):
                rounded.append(self.normalised(inv, m))
        return jnp.dot(jnp.concatenate(rounded, axis=1), matrix, preferred_element_type=F32)

    def near_halo(self, zown, zy, matrix):
        return self.halo([zown[0], zown[1], zy[0], zy[1]], matrix[0:4 * 128, :], True)

    def far_halo(self, xlo, xhi, matrix):
        tiles = [jnp.where(self.lane >= 64, xlo[2 * E + i].astype(F32), xhi[2 * E + i].astype(F32)).astype(BF16)
                 for i in range(2)]
        return self.halo(tiles, matrix[4 * 128:6 * 128, :], False)

    def halo_of(self, windows, c):
        half = windows[:, c // 32 * 128:c // 32 * 128 + 128]
        turned = pltpu.roll(half, (126 - 4 * (c % 32)) % 128, 1)
        return jnp.where((self.lane < 2) | (self.lane >= 126), turned, 0.0)

    def back(self, x, boxes, inv, own, memb=None):
        ws, ms = [], []
        for y in range(W):
            prod = inv(y) * boxes[y]
            m = prod * recip(jnp.sum(prod, axis=0, keepdims=True))
            ms.append(m)
            ws.append((m * m).astype(BF16))
        if memb is not None:
            for g in range(4):
                for k, rows in enumerate(turned8([m[8 * g:8 * g + 8] for m in ms])):
                    memb[8 * g + k, x] = rows
        w = jnp.concatenate(ws, axis=1)
        t = jnp.concatenate([own[x * W + y] for y in range(W)], axis=1)
        self.numer = self.numer + dot_lanes(w, t)
        self.denom = self.denom + dot_lanes(jnp.ones((8, W * 128), BF16), w)


def total(arrays):
    out = arrays[0]
    for a in arrays[1:]:
        out = out + a
    return out


def mid_column(own, ylo, yhi):
    def column(X, Y):
        x = X - 2
        if Y < 2:
            return ylo[x * 2 + Y]
        if Y >= W + 2:
            return yhi[x * 2 + Y - W - 2]
        return own[x * W + Y - 2]
    return column


def outer_column(xlo, xhi):
    def column(X, Y):
        ref, i = (xlo, X) if X < 2 else (xhi, X - W - 2)
        if Y < 2:
            return ref[16 + i * 2 + Y]
        if Y >= W + 2:
            return ref[20 + i * 2 + Y - W - 2]
        return ref[i * W + Y - 2]
    return column


def inner_kernel(own, ylo, yhi, zown, zy, matrix, cent, edge, box, kept, sums, inv_s, win_s):
    step = Step(cent, edge)
    column = mid_column(own, ylo, yhi)
    windows = step.near_halo(zown, zy, matrix)
    for x in range(W):
        def keep(y, inv, x=x):
            if x in INNER:
                inv_s[(x - 2) * W + y] = inv
            else:
                kept[OUTER.index(x) * W + y] = inv
        for y, w in enumerate(step.front(x + 2, column, keep)):
            win_s[x * W + y] = w

    def mid_box(x, y):
        rows = range(max(x - 2, 0), min(x + 3, W))
        return total([win_s[r * W + y] for r in rows]) + step.halo_of(windows, x * W + y)

    for x in INNER:
        step.back(x, [mid_box(x, y) for y in range(W)], lambda y: inv_s[(x - 2) * W + y], own)
    for i, x in enumerate(OUTER):
        for y in range(W):
            box[i * W + y] = mid_box(x, y)
    sums[0:F, :] = step.numer
    sums[F:F + 8, :] = step.denom


def outer_kernel(own, xlo, xhi, matrix, cent, edge, box, kept, sums, part, win_s):
    step = Step(cent, edge)
    column = outer_column(xlo, xhi)
    windows = step.far_halo(xlo, xhi, matrix)
    for i, X in enumerate(ROWS):
        for y, w in enumerate(step.front(X, column, None)):
            win_s[i * W + y] = w
    for i, x in enumerate(OUTER):
        near = [n for n, X in enumerate(ROWS) if x <= X <= x + 4]
        boxes = [
            total([box[i * W + y]] + [win_s[n * W + y] for n in near])
            + step.halo_of(windows, x * W + y)
            for y in range(W)
        ]
        step.back(x, boxes, lambda y: kept[i * W + y], own)
    store_sums(part, step.numer + sums[0:F, :], step.denom + sums[F:F + 8, :])


def whole_kernel(own, ylo, yhi, xlo, xhi, zown, zy, matrix, cent, edge, memb, part, inv_s, win_s):
    step = Step(cent, edge)
    mid, outer = mid_column(own, ylo, yhi), outer_column(xlo, xhi)
    windows = step.near_halo(zown, zy, matrix) + step.far_halo(xlo, xhi, matrix)
    for X in range(E):
        def keep(y, inv, X=X):
            inv_s[(X - 2) * W + y] = inv
        for y, w in enumerate(step.front(X, mid if 2 <= X < W + 2 else outer, keep)):
            win_s[X * W + y] = w
    for x in range(W):
        boxes = [
            total([win_s[X * W + y] for X in range(x, x + 5)]) + step.halo_of(windows, x * W + y)
            for y in range(W)
        ]
        step.back(x, boxes, lambda y: inv_s[x * W + y], own, memb)
    store_sums(part, step.numer, step.denom)


VMEM = pl.BlockSpec(memory_space=pltpu.VMEM)
ANY = pl.BlockSpec(memory_space=pl.ANY)


def call(kernel, out_shape, in_specs, scratch_shapes, flops, moved, args):
    return pl.pallas_call(
        kernel,
        out_shape=tuple(jax.ShapeDtypeStruct(s, t) for s, t in out_shape),
        in_specs=in_specs,
        out_specs=(VMEM,) * len(out_shape),
        scratch_shapes=scratch_shapes,
        compiler_params=pltpu.CompilerParams(vmem_limit_bytes=24 << 20),
        cost_estimate=pl.CostEstimate(flops=flops, bytes_accessed=moved, transcendentals=0),
    )(*args)


def columns(n, dtype=F32):
    return (n, F, 128), dtype


def prepare(attributes, start):
    return call(
        prepare_kernel, [columns(COLS, BF16), columns(2, BF16), ((9, 128), F32)], [ANY] * 2,
        [pltpu.VMEM(attributes.shape, BF16), pltpu.VMEM(start.shape, F32),
         pltpu.SemaphoreType.DMA((3,))],
        10 ** 6, 1 << 20,
        [pltpu.with_memory_space_constraint(a, pltpu.HBM) for a in (attributes, start)])


def inner_part(own, ylo, yhi, zown, zy, matrix, cent, edge):
    return call(
        inner_kernel, [columns(4 * W), columns(4 * W), ((F + 8, F), F32)], [VMEM] * 8,
        [pltpu.VMEM(*columns(4 * W)), pltpu.VMEM(*columns(COLS))],
        5 * 10 ** 8, 3 << 20, (own, ylo, yhi, zown, zy, matrix, cent, edge))


def outer_part(own, xlo, xhi, matrix, cent, edge, box, kept, sums):
    return call(
        outer_kernel, [((9, 128), F32)], [VMEM] * 9,
        [pltpu.VMEM(*columns(4 * W))],
        2 * 10 ** 8, 2 << 20, (own, xlo, xhi, matrix, cent, edge, box, kept, sums))[0]


def whole_update(own, ylo, yhi, xlo, xhi, zown, zy, matrix, cent, edge):
    return call(
        whole_kernel, [((F, W, W, 128), F32), ((9, 128), F32)], [VMEM] * 10,
        [pltpu.VMEM(*columns(COLS)), pltpu.VMEM(*columns(E * W))],
        8 * 10 ** 8, 3 << 20, (own, ylo, yhi, xlo, xhi, zown, zy, matrix, cent, edge))


def both_ways(up, down, axes, count):
    lo = lax.ppermute(up, axes, [(i, (i + 1) % count) for i in range(count)])
    hi = lax.ppermute(down, axes, [((i + 1) % count, i) for i in range(count)])
    return lo, hi


def gather_sum(part, axes, count):
    every = lax.all_to_all(jnp.broadcast_to(part[None], (count,) + part.shape), axes, 0, 0)
    return jnp.sum(every, axis=0)


def total_sums(part):
    part = gather_sum(part.reshape(9, 1, 128), ("core", "gz"), 16)
    return gather_sum(part, ("cx", "gy"), 16).reshape(9, 128)


def edges():
    gx, gy, gz = lax.axis_index(XS), lax.axis_index("gy"), lax.axis_index("gz")
    row = lax.broadcasted_iota(jnp.int32, (8, 128), 0)
    inside = jnp.zeros((8, 128), jnp.bool_)
    for i, has in enumerate((gx > 0, gx < 7, gy > 0, gy < 3, gz > 0, gz < 7)):
        inside = inside | ((row == i) & has)
    return inside.astype(F32)


def per_device(attributes, start_centroids):
    edge = edges()
    matrix = jnp.asarray(halo_matrix(), BF16)
    lane = lax.broadcasted_iota(jnp.int32, (1, 1, 128), 2)
    own, ends, cent = prepare(attributes, start_centroids)
    grid = own.reshape(W, W, F, 128)
    ylo, yhi = both_ways(
        grid[:, W - 2:].reshape(2 * W, F, 128), grid[:, :2].reshape(2 * W, F, 128), "gy", 4)
    zlo, zhi = both_ways(ends, ends, "gz", 8)
    zown = jnp.where(lane % 4 < 2, zlo, zhi)
    zylo, zyhi = both_ways(zown, zown, "gy", 4)
    zy = jnp.where(lane // 4 % W >= W // 2, zylo, zyhi)

    def x_slice(x, half):
        return jnp.concatenate(
            [own[x * W:x * W + 2 * W], ylo[2 * x:2 * x + 4], yhi[2 * x:2 * x + 4],
             zown[half:half + 1], zy[half:half + 1]])

    xlo, xhi = both_ways(x_slice(W - 2, 1), x_slice(0, 0), XS, 8)

    box, kept, sums = inner_part(own, ylo, yhi, zown, zy, matrix, cent, edge)
    part = outer_part(own, xlo, xhi, matrix, cent, edge, box, kept, sums)
    cent = total_sums(part)
    memb, part = whole_update(own, ylo, yhi, xlo, xhi, zown, zy, matrix, cent, edge)
    cent = total_sums(part)
    numer = cent[:8].reshape(8, 4, F).transpose(1, 0, 2).reshape(F, F)
    return numer / cent[8, :F][:, None], memb


def solution(mesh):
    split = Mesh(np.asarray(mesh.devices).reshape(4, 2, 4, 8), ("cx", "core", "gy", "gz"))
    return jax.shard_map(
        per_device,
        mesh=split,
        in_specs=(P(None, XS, "gy", "gz"), P()),
        out_specs=(P(), P(None, XS, "gy", "gz")),
        check_vma=False,
    )
```

```python
import jax
import jax.numpy as jnp
import numpy as np
from jax import lax
from jax.experimental import pallas as pl
from jax.experimental.pallas import tpu as pltpu
from jax.sharding import Mesh, PartitionSpec as P

F = 32
W = 8
E = W + 4
COLS = W * W
BF16 = jnp.bfloat16
F32 = jnp.float32
XS = ("cx", "core")
OUTER = (0, 1, W - 2, W - 1)
INNER = tuple(range(2, W - 2))
ROWS = (0, 1, W + 2, W + 3)


def tile_columns():
    def beyond(i):
        return i - W if i >= W // 2 else i + W

    own = [(c // W, c % W) for c in range(COLS)]
    ys = [(x, beyond(y)) for x, y in own]
    xs = [(beyond(j // W + (4 if j >= 16 else 0)), j % W) for j in range(32)]
    return own + ys + xs + [(x, beyond(y)) for x, y in xs]


def halo_matrix():
    src = [(x, y, z) for x, y in tile_columns() for z in (-2, -1, 128, 129)]
    dst = [(c // W, c % W, z) for c in range(COLS) for z in (126, 127, 0, 1)]
    gap = np.abs(np.array(src)[:, None, :] - np.array(dst)[None, :, :])
    return (gap <= 2).all(-1).astype(np.float32)


def band_matrix():
    gap = lax.broadcasted_iota(jnp.int32, (128, 128), 0) - lax.broadcasted_iota(jnp.int32, (128, 128), 1)
    return jnp.where(jnp.abs(gap) <= 2, 1.0, 0.0).astype(BF16)


def recip(x):
    return pl.reciprocal(x, approx=True)


def dot_lanes(a, b):
    return lax.dot_general(a, b, (((1,), (1,)), ((), ())), preferred_element_type=F32)


def unpacked_centroids(sums):
    lane = lax.broadcasted_iota(jnp.int32, (8, 128), 1)
    row = lax.broadcasted_iota(jnp.int32, (8, 128), 0)
    denom = jnp.broadcast_to(sums[8:9, :], (8, 128))
    parts = []
    for g in range(4):
        d = jnp.sum(jnp.where(lane == row + 8 * g, denom, 0.0), axis=1, keepdims=True)
        parts.append(sums[0:8, 32 * g:32 * g + 32] / d)
    return jnp.concatenate(parts, axis=0)


def store_sums(part, numer, denom):
    packed = jnp.concatenate([numer[8 * g:8 * g + 8] for g in range(4)], axis=1)
    part[...] = jnp.concatenate([packed, jnp.concatenate([denom] * 4, axis=1)], axis=0).astype(BF16)


def turned8(v):
    row = lax.broadcasted_iota(jnp.int32, (8, 128), 0)
    v = list(v)
    for s in (4, 2, 1):
        low = (row & s) == 0
        for i in range(8):
            if not i & s:
                a, b = v[i], v[i + s]
                v[i] = jnp.where(low, a, pltpu.roll(b, s, 0))
                v[i + s] = jnp.where(low, pltpu.roll(a, 8 - s, 0), b)
    return v


def prepare_kernel(attr_hbm, start_hbm, own, ends, cent, attr, start, sems):
    fetch = [
        pltpu.make_async_copy(attr_hbm.at[:, x:x + 4], attr.at[:, x:x + 4], sems.at[x // 4])
        for x in range(0, W, 4)
    ]
    fetch.append(pltpu.make_async_copy(start_hbm, start, sems.at[2]))
    for f in fetch:
        f.start()
    lane = lax.broadcasted_iota(jnp.int32, (1, 128), 1) // 4
    for half in range(2):
        acc = jnp.zeros((F, 128), F32)
        fetch[half].wait()
        for x in range(half * 4, half * 4 + 4):
            wide = [attr[a, x].astype(F32) for a in range(F)]
            groups = [turned8(wide[8 * g:8 * g + 8]) for g in range(4)]
            for y in range(W):
                c = x * W + y
                j = c % 32
                col = jnp.concatenate([groups[g][y] for g in range(4)], axis=0)
                own[c] = col.astype(BF16)
                acc = jnp.where(lane == j, pltpu.roll(col, (4 * j + 2) % 128, 1), acc)
        ends[half] = acc.astype(BF16)
    fetch[-1].wait()
    cent[0:8, :] = jnp.concatenate([start[8 * g:8 * g + 8, :] for g in range(4)], axis=1)
    cent[8:9, :] = jnp.ones((1, 128), F32)


class Step:
    def __init__(self, cent, edge):
        c = unpacked_centroids(cent)
        self.cbm2 = (-2.0 * c.astype(BF16).astype(F32)).astype(BF16)
        self.csq1 = jnp.broadcast_to(jnp.sum(c * c, axis=1, keepdims=True) + 1.0, (F, 128))
        self.xlo, self.xhi, self.ylo, self.yhi, self.zlo, self.zhi = [edge[i:i + 1, :] for i in range(6)]
        self.band = band_matrix()
        self.lane = lax.broadcasted_iota(jnp.int32, (1, 128), 1)
        self.numer = jnp.zeros((F, F), F32)
        self.ends = jnp.where((self.lane < 2) | (self.lane >= 126), 1.0, 0.0)
        self.denom = jnp.zeros((8, F), F32)

    def inverse(self, a):
        af = a.astype(F32)
        sq = jnp.sum(af * af, axis=0, keepdims=True)
        cross = jnp.dot(self.cbm2, a, preferred_element_type=F32)
        return [
            recip(cross[:, s:s + 128] + self.csq1 + sq[:, s:s + 128])
            for s in range(0, a.shape[1], 128)
        ]

    def normalised(self, inv, mask):
        scale = recip(jnp.sum(inv, axis=0, keepdims=True))
        if mask is not None:
            scale = scale * mask
        return (inv * scale).astype(BF16)

    def front(self, X, column, keep):
        mx = self.xlo if X < 2 else (self.xhi if X >= W + 2 else None)
        rounded = []
        for Y in range(0, E, 2):
            my = self.ylo if Y < 2 else (self.yhi if Y >= W + 2 else None)
            m = mx if my is None else (my if mx is None else mx * my)
            pair = jnp.concatenate([column(X, Y), column(X, Y + 1)], axis=1)
            for i, inv in enumerate(self.inverse(pair)):
                if mx is None and my is None:
                    keep(Y + i - 2, inv)
                rounded.append(self.normalised(inv, m))
        z = jnp.dot(jnp.concatenate(rounded, axis=0), self.band, preferred_element_type=F32)
        cols = [z[F * Y:F * Y + F] for Y in range(E)]
        p = [cols[Y] + cols[Y + 1] for Y in range(E - 1)]
        return [p[y] + p[y + 2] + cols[y + 4] for y in range(W)]

    def halo(self, tiles, matrix, near):
        j = self.lane // 4
        mz = jnp.where(self.lane % 4 < 2, self.zlo, self.zhi)
        my = mz * jnp.where(j % W >= W // 2, self.ylo, self.yhi)
        mx = jnp.where(j >= 16, self.xlo, self.xhi)
        masks = [mz, mz, my, my] if near else [mz * mx, my * mx]
        rounded = []
        for i in range(0, len(tiles), 2):
            pair = jnp.concatenate([tiles[i], tiles[i + 1]], axis=1)
            for inv, m in zip(self.inverse(pair), masks[i:i + 2]):
                rounded.append(self.normalised(inv, m))
        return jnp.dot(jnp.concatenate(rounded, axis=1), matrix, preferred_element_type=F32)

    def near_halo(self, zown, zy, matrix):
        return self.halo([zown[0], zown[1], zy[0], zy[1]], matrix[0:4 * 128, :], True)

    def far_halo(self, xlo, xhi, matrix):
        tiles = [jnp.where(self.lane >= 64, xlo[2 * E + i].astype(F32), xhi[2 * E + i].astype(F32)).astype(BF16)
                 for i in range(2)]
        return self.halo(tiles, matrix[4 * 128:6 * 128, :], False)

    def halo_of(self, windows, c):
        half = windows[:, c // 32 * 128:c // 32 * 128 + 128]
        turned = pltpu.roll(half, (126 - 4 * (c % 32)) % 128, 1)
        return turned * self.ends

    def back(self, x, boxes, inv, own, memb=None):
        ws, ms = [], []
        for y in range(W):
            prod = inv(y) * boxes[y]
            m = prod * recip(jnp.sum(prod, axis=0, keepdims=True))
            ms.append(m)
            ws.append((m * m).astype(BF16))
        if memb is not None:
            for g in range(4):
                for k, rows in enumerate(turned8([m[8 * g:8 * g + 8] for m in ms])):
                    memb[8 * g + k, x] = rows
        w = jnp.concatenate(ws, axis=1)
        t = jnp.concatenate([own[x * W + y] for y in range(W)], axis=1)
        self.numer = self.numer + dot_lanes(w, t)
        self.denom = self.denom + dot_lanes(jnp.ones((8, W * 128), BF16), w)


def total(arrays):
    out = arrays[0]
    for a in arrays[1:]:
        out = out + a
    return out


def mid_column(own, ylo, yhi):
    def column(X, Y):
        x = X - 2
        if Y < 2:
            return ylo[x * 2 + Y]
        if Y >= W + 2:
            return yhi[x * 2 + Y - W - 2]
        return own[x * W + Y - 2]
    return column


def outer_column(xlo, xhi):
    def column(X, Y):
        ref, i = (xlo, X) if X < 2 else (xhi, X - W - 2)
        if Y < 2:
            return ref[16 + i * 2 + Y]
        if Y >= W + 2:
            return ref[20 + i * 2 + Y - W - 2]
        return ref[i * W + Y - 2]
    return column


def inner_kernel(own, ylo, yhi, zown, zy, matrix, cent, edge, box, kept, sums, inv_s, win_s):
    step = Step(cent, edge)
    column = mid_column(own, ylo, yhi)
    windows = step.near_halo(zown, zy, matrix)
    for x in range(W):
        def keep(y, inv, x=x):
            if x in INNER:
                inv_s[(x - 2) * W + y] = inv
            else:
                kept[OUTER.index(x) * W + y] = inv
        for y, w in enumerate(step.front(x + 2, column, keep)):
            win_s[x * W + y] = w

    def mid_box(x, y):
        rows = range(max(x - 2, 0), min(x + 3, W))
        return total([win_s[r * W + y] for r in rows]) + step.halo_of(windows, x * W + y)

    for x in INNER:
        step.back(x, [mid_box(x, y) for y in range(W)], lambda y: inv_s[(x - 2) * W + y], own)
    for i, x in enumerate(OUTER):
        for y in range(W):
            box[i * W + y] = mid_box(x, y)
    sums[0:F, :] = step.numer
    sums[F:F + 8, :] = step.denom


def outer_kernel(own, xlo, xhi, matrix, cent, edge, box, kept, sums, part, win_s):
    step = Step(cent, edge)
    column = outer_column(xlo, xhi)
    windows = step.far_halo(xlo, xhi, matrix)
    for i, X in enumerate(ROWS):
        for y, w in enumerate(step.front(X, column, None)):
            win_s[i * W + y] = w
    for i, x in enumerate(OUTER):
        near = [n for n, X in enumerate(ROWS) if x <= X <= x + 4]
        boxes = [
            total([box[i * W + y]] + [win_s[n * W + y] for n in near])
            + step.halo_of(windows, x * W + y)
            for y in range(W)
        ]
        step.back(x, boxes, lambda y: kept[i * W + y], own)
    store_sums(part, step.numer + sums[0:F, :], step.denom + sums[F:F + 8, :])


def whole_kernel(own, ylo, yhi, xlo, xhi, zown, zy, matrix, cent, edge, memb, part, inv_s, win_s):
    step = Step(cent, edge)
    mid, outer = mid_column(own, ylo, yhi), outer_column(xlo, xhi)
    windows = step.near_halo(zown, zy, matrix) + step.far_halo(xlo, xhi, matrix)
    for X in range(E):
        def keep(y, inv, X=X):
            inv_s[(X - 2) * W + y] = inv
        for y, w in enumerate(step.front(X, mid if 2 <= X < W + 2 else outer, keep)):
            win_s[X * W + y] = w
    for x in range(W):
        boxes = [
            total([win_s[X * W + y] for X in range(x, x + 5)]) + step.halo_of(windows, x * W + y)
            for y in range(W)
        ]
        step.back(x, boxes, lambda y: inv_s[x * W + y], own, memb)
    store_sums(part, step.numer, step.denom)


VMEM = pl.BlockSpec(memory_space=pltpu.VMEM)
ANY = pl.BlockSpec(memory_space=pl.ANY)


def call(kernel, out_shape, in_specs, scratch_shapes, flops, moved, args):
    return pl.pallas_call(
        kernel,
        out_shape=tuple(jax.ShapeDtypeStruct(s, t) for s, t in out_shape),
        in_specs=in_specs,
        out_specs=(VMEM,) * len(out_shape),
        scratch_shapes=scratch_shapes,
        compiler_params=pltpu.CompilerParams(vmem_limit_bytes=24 << 20),
        cost_estimate=pl.CostEstimate(flops=flops, bytes_accessed=moved, transcendentals=0),
    )(*args)


def columns(n, dtype=F32):
    return (n, F, 128), dtype


def prepare(attributes, start):
    return call(
        prepare_kernel, [columns(COLS, BF16), columns(2, BF16), ((9, 128), F32)], [ANY] * 2,
        [pltpu.VMEM(attributes.shape, BF16), pltpu.VMEM(start.shape, F32),
         pltpu.SemaphoreType.DMA((3,))],
        10 ** 6, 1 << 20,
        [pltpu.with_memory_space_constraint(a, pltpu.HBM) for a in (attributes, start)])


def inner_part(own, ylo, yhi, zown, zy, matrix, cent, edge):
    return call(
        inner_kernel, [columns(4 * W), columns(4 * W), ((F + 8, F), F32)], [VMEM] * 8,
        [pltpu.VMEM(*columns(4 * W)), pltpu.VMEM(*columns(COLS))],
        5 * 10 ** 8, 3 << 20, (own, ylo, yhi, zown, zy, matrix, cent, edge))


def outer_part(own, xlo, xhi, matrix, cent, edge, box, kept, sums):
    return call(
        outer_kernel, [((16, 128), BF16)], [VMEM] * 9,
        [pltpu.VMEM(*columns(4 * W))],
        2 * 10 ** 8, 2 << 20, (own, xlo, xhi, matrix, cent, edge, box, kept, sums))[0]


def whole_update(own, ylo, yhi, xlo, xhi, zown, zy, matrix, cent, edge):
    return call(
        whole_kernel, [((F, W, W, 128), F32), ((16, 128), BF16)], [VMEM] * 10,
        [pltpu.VMEM(*columns(COLS)), pltpu.VMEM(*columns(E * W))],
        8 * 10 ** 8, 3 << 20, (own, ylo, yhi, xlo, xhi, zown, zy, matrix, cent, edge))


def both_ways(up, down, axes, count):
    lo = lax.ppermute(up, axes, [(i, (i + 1) % count) for i in range(count)])
    hi = lax.ppermute(down, axes, [((i + 1) % count, i) for i in range(count)])
    return lo, hi


def gather_sum(part, axes, count):
    every = lax.all_to_all(jnp.broadcast_to(part[None], (count,) + part.shape), axes, 0, 0)
    return jnp.sum(every.astype(F32), axis=0)


def total_sums(part):
    part = gather_sum(part[:10].reshape(5, 2, 128), ("core", "gz"), 16)
    return gather_sum(part.reshape(10, 1, 128)[:9], ("cx", "gy"), 16).reshape(9, 128)


def edges():
    gx, gy, gz = lax.axis_index(XS), lax.axis_index("gy"), lax.axis_index("gz")
    row = lax.broadcasted_iota(jnp.int32, (8, 128), 0)
    inside = jnp.zeros((8, 128), jnp.bool_)
    for i, has in enumerate((gx > 0, gx < 7, gy > 0, gy < 3, gz > 0, gz < 7)):
        inside = inside | ((row == i) & has)
    return inside.astype(F32)


def per_device(attributes, start_centroids):
    edge = edges()
    matrix = jnp.asarray(halo_matrix(), BF16)
    lane = lax.broadcasted_iota(jnp.int32, (1, 1, 128), 2)
    own, ends, cent = prepare(attributes, start_centroids)
    grid = own.reshape(W, W, F, 128)
    ylo, yhi = both_ways(
        grid[:, W - 2:].reshape(2 * W, F, 128), grid[:, :2].reshape(2 * W, F, 128), "gy", 4)
    zlo, zhi = both_ways(ends, ends, "gz", 8)
    zown = jnp.where(lane % 4 < 2, zlo, zhi)
    zylo, zyhi = both_ways(zown, zown, "gy", 4)
    zy = jnp.where(lane // 4 % W >= W // 2, zylo, zyhi)

    def x_slice(x, half):
        return jnp.concatenate(
            [own[x * W:x * W + 2 * W], ylo[2 * x:2 * x + 4], yhi[2 * x:2 * x + 4],
             zown[half:half + 1], zy[half:half + 1]])

    xlo, xhi = both_ways(x_slice(W - 2, 1), x_slice(0, 0), XS, 8)

    box, kept, sums = inner_part(own, ylo, yhi, zown, zy, matrix, cent, edge)
    part = outer_part(own, xlo, xhi, matrix, cent, edge, box, kept, sums)
    cent = total_sums(part)
    memb, part = whole_update(own, ylo, yhi, xlo, xhi, zown, zy, matrix, cent, edge)
    cent = total_sums(part)
    numer = cent[:8].reshape(8, 4, F).transpose(1, 0, 2).reshape(F, F)
    return numer / cent[8, :F][:, None], memb


def solution(mesh):
    split = Mesh(np.asarray(mesh.devices).reshape(4, 2, 4, 8), ("cx", "core", "gy", "gz"))
    return jax.shard_map(
        per_device,
        mesh=split,
        in_specs=(P(None, XS, "gy", "gz"), P()),
        out_specs=(P(), P(None, XS, "gy", "gz")),
        check_vma=False,
    )
```

```python
import jax
import jax.numpy as jnp
import numpy as np
from jax import lax
from jax.experimental import pallas as pl
from jax.experimental.pallas import tpu as pltpu
from jax.sharding import Mesh, PartitionSpec as P

F = 32
W = 8
E = W + 4
COLS = W * W
BF16 = jnp.bfloat16
F32 = jnp.float32
XS = ("cx", "core")
OUTER = (0, 1, W - 2, W - 1)
INNER = tuple(range(2, W - 2))
ROWS = (0, 1, W + 2, W + 3)


def tile_columns():
    def beyond(i):
        return i - W if i >= W // 2 else i + W

    own = [(c // W, c % W) for c in range(COLS)]
    ys = [(x, beyond(y)) for x, y in own]
    xs = [(beyond(j // W + (4 if j >= 16 else 0)), j % W) for j in range(32)]
    return own + ys + xs + [(x, beyond(y)) for x, y in xs]


def halo_matrix():
    src = [(x, y, z) for x, y in tile_columns() for z in (-2, -1, 128, 129)]
    dst = [(c // W, c % W, z) for c in range(COLS) for z in (126, 127, 0, 1)]
    gap = np.abs(np.array(src)[:, None, :] - np.array(dst)[None, :, :])
    return (gap <= 2).all(-1).astype(np.float32)


def band_matrix():
    gap = lax.broadcasted_iota(jnp.int32, (128, 128), 0) - lax.broadcasted_iota(jnp.int32, (128, 128), 1)
    return jnp.where(jnp.abs(gap) <= 2, 1.0, 0.0).astype(BF16)


def recip(x):
    return pl.reciprocal(x, approx=True)


def dot_lanes(a, b):
    return lax.dot_general(a, b, (((1,), (1,)), ((), ())), preferred_element_type=F32)


def unpacked_centroids(sums):
    lane = lax.broadcasted_iota(jnp.int32, (8, 128), 1)
    row = lax.broadcasted_iota(jnp.int32, (8, 128), 0)
    denom = jnp.broadcast_to(sums[8:9, :], (8, 128))
    parts = []
    for g in range(4):
        d = jnp.sum(jnp.where(lane == row + 8 * g, denom, 0.0), axis=1, keepdims=True)
        parts.append(sums[0:8, 32 * g:32 * g + 32] / d)
    return jnp.concatenate(parts, axis=0)


def store_sums(part, numer, denom):
    packed = jnp.concatenate([numer[8 * g:8 * g + 8] for g in range(4)], axis=1)
    part[...] = jnp.concatenate([packed, jnp.concatenate([denom] * 4, axis=1)], axis=0).astype(BF16)


def turned8(v):
    row = lax.broadcasted_iota(jnp.int32, (8, 128), 0)
    v = list(v)
    for s in (4, 2, 1):
        low = (row & s) == 0
        for i in range(8):
            if not i & s:
                a, b = v[i], v[i + s]
                v[i] = jnp.where(low, a, pltpu.roll(b, s, 0))
                v[i + s] = jnp.where(low, pltpu.roll(a, 8 - s, 0), b)
    return v


def prepare_kernel(attr_hbm, start_hbm, own, ends, cent, attr, start, sems):
    fetch = [
        pltpu.make_async_copy(attr_hbm.at[:, x:x + 4], attr.at[:, x:x + 4], sems.at[x // 4])
        for x in range(0, W, 4)
    ]
    fetch.append(pltpu.make_async_copy(start_hbm, start, sems.at[2]))
    for f in fetch:
        f.start()
    lane = lax.broadcasted_iota(jnp.int32, (1, 128), 1) // 4
    for half in range(2):
        acc = jnp.zeros((F, 128), F32)
        fetch[half].wait()
        for x in range(half * 4, half * 4 + 4):
            wide = [attr[a, x].astype(F32) for a in range(F)]
            groups = [turned8(wide[8 * g:8 * g + 8]) for g in range(4)]
            for y in range(W):
                c = x * W + y
                j = c % 32
                col = jnp.concatenate([groups[g][y] for g in range(4)], axis=0)
                own[c] = col.astype(BF16)
                acc = jnp.where(lane == j, pltpu.roll(col, (4 * j + 2) % 128, 1), acc)
        ends[half] = acc.astype(BF16)
    fetch[-1].wait()
    cent[0:8, :] = jnp.concatenate([start[8 * g:8 * g + 8, :] for g in range(4)], axis=1)
    cent[8:9, :] = jnp.ones((1, 128), F32)


class Step:
    def __init__(self, cent, edge):
        c = unpacked_centroids(cent)
        self.cbm2 = (-2.0 * c.astype(BF16).astype(F32)).astype(BF16)
        self.csq1 = jnp.broadcast_to(jnp.sum(c * c, axis=1, keepdims=True) + 1.0, (F, 128))
        self.xlo, self.xhi, self.ylo, self.yhi, self.zlo, self.zhi = [edge[i:i + 1, :] for i in range(6)]
        self.band = band_matrix()
        self.lane = lax.broadcasted_iota(jnp.int32, (1, 128), 1)
        self.numer = jnp.zeros((F, F), F32)
        self.ends = jnp.where((self.lane < 2) | (self.lane >= 126), 1.0, 0.0)
        self.denom = jnp.zeros((8, F), F32)

    def inverse(self, a):
        af = a.astype(F32)
        sq = jnp.sum(af * af, axis=0, keepdims=True)
        cross = jnp.dot(self.cbm2, a, preferred_element_type=F32)
        return [
            recip(cross[:, s:s + 128] + self.csq1 + sq[:, s:s + 128])
            for s in range(0, a.shape[1], 128)
        ]

    def normalised(self, inv, mask):
        scale = recip(jnp.sum(inv, axis=0, keepdims=True))
        if mask is not None:
            scale = scale * mask
        return (inv * scale).astype(BF16)

    def front(self, X, column, keep):
        mx = self.xlo if X < 2 else (self.xhi if X >= W + 2 else None)
        rounded = []
        for Y in range(0, E, 2):
            my = self.ylo if Y < 2 else (self.yhi if Y >= W + 2 else None)
            m = mx if my is None else (my if mx is None else mx * my)
            pair = jnp.concatenate([column(X, Y), column(X, Y + 1)], axis=1)
            for i, inv in enumerate(self.inverse(pair)):
                if mx is None and my is None:
                    keep(Y + i - 2, inv)
                rounded.append(self.normalised(inv, m))
        z = jnp.dot(jnp.concatenate(rounded, axis=0), self.band, preferred_element_type=F32)
        cols = [z[F * Y:F * Y + F] for Y in range(E)]
        p = [cols[Y] + cols[Y + 1] for Y in range(E - 1)]
        return [p[y] + p[y + 2] + cols[y + 4] for y in range(W)]

    def halo(self, tiles, matrix, near):
        j = self.lane // 4
        mz = jnp.where(self.lane % 4 < 2, self.zlo, self.zhi)
        my = mz * jnp.where(j % W >= W // 2, self.ylo, self.yhi)
        mx = jnp.where(j >= 16, self.xlo, self.xhi)
        masks = [mz, mz, my, my] if near else [mz * mx, my * mx]
        rounded = []
        for i in range(0, len(tiles), 2):
            pair = jnp.concatenate([tiles[i], tiles[i + 1]], axis=1)
            for inv, m in zip(self.inverse(pair), masks[i:i + 2]):
                rounded.append(self.normalised(inv, m))
        return jnp.dot(jnp.concatenate(rounded, axis=1), matrix, preferred_element_type=F32)

    def near_halo(self, zown, zy, matrix):
        return self.halo([zown[0], zown[1], zy[0], zy[1]], matrix[0:4 * 128, :], True)

    def far_halo(self, xlo, xhi, matrix):
        tiles = [jnp.where(self.lane >= 64, xlo[2 * E + i].astype(F32), xhi[2 * E + i].astype(F32)).astype(BF16)
                 for i in range(2)]
        return self.halo(tiles, matrix[4 * 128:6 * 128, :], False)

    def halo_of(self, windows, c):
        half = windows[:, c // 32 * 128:c // 32 * 128 + 128]
        turned = pltpu.roll(half, (126 - 4 * (c % 32)) % 128, 1)
        return turned * self.ends

    def back(self, x, boxes, inv, own, memb=None):
        ws, ms = [], []
        for y in range(W):
            prod = inv(y) * boxes[y]
            m = prod * recip(jnp.sum(prod, axis=0, keepdims=True))
            ms.append(m)
            ws.append((m * m).astype(BF16))
        if memb is not None:
            for g in range(4):
                for k, rows in enumerate(turned8([m[8 * g:8 * g + 8] for m in ms])):
                    memb[8 * g + k, x] = rows
        w = jnp.concatenate(ws, axis=1)
        t = jnp.concatenate([own[x * W + y] for y in range(W)], axis=1)
        self.numer = self.numer + dot_lanes(w, t)
        self.denom = self.denom + dot_lanes(jnp.ones((8, W * 128), BF16), w)


def total(arrays):
    out = arrays[0]
    for a in arrays[1:]:
        out = out + a
    return out


def mid_column(own, ylo, yhi):
    def column(X, Y):
        x = X - 2
        if Y < 2:
            return ylo[x * 2 + Y]
        if Y >= W + 2:
            return yhi[x * 2 + Y - W - 2]
        return own[x * W + Y - 2]
    return column


def outer_column(xlo, xhi):
    def column(X, Y):
        ref, i = (xlo, X) if X < 2 else (xhi, X - W - 2)
        if Y < 2:
            return ref[16 + i * 2 + Y]
        if Y >= W + 2:
            return ref[20 + i * 2 + Y - W - 2]
        return ref[i * W + Y - 2]
    return column


def inner_kernel(own, ylo, yhi, zown, zy, matrix, cent, edge, box, kept, sums, inv_s, win_s):
    step = Step(cent, edge)
    column = mid_column(own, ylo, yhi)
    windows = step.near_halo(zown, zy, matrix)
    for x in range(W):
        def keep(y, inv, x=x):
            if x in INNER:
                inv_s[(x - 2) * W + y] = inv
            else:
                kept[OUTER.index(x) * W + y] = inv
        for y, w in enumerate(step.front(x + 2, column, keep)):
            win_s[x * W + y] = w

    def mid_box(x, y):
        rows = range(max(x - 2, 0), min(x + 3, W))
        return total([win_s[r * W + y] for r in rows]) + step.halo_of(windows, x * W + y)

    for x in INNER:
        step.back(x, [mid_box(x, y) for y in range(W)], lambda y: inv_s[(x - 2) * W + y], own)
    for i, x in enumerate(OUTER):
        for y in range(W):
            box[i * W + y] = mid_box(x, y)
    sums[0:F, :] = step.numer
    sums[F:F + 8, :] = step.denom


def outer_kernel(own, xlo, xhi, matrix, cent, edge, box, kept, sums, part, win_s):
    step = Step(cent, edge)
    column = outer_column(xlo, xhi)
    windows = step.far_halo(xlo, xhi, matrix)
    for i, X in enumerate(ROWS):
        for y, w in enumerate(step.front(X, column, None)):
            win_s[i * W + y] = w
    for i, x in enumerate(OUTER):
        near = [n for n, X in enumerate(ROWS) if x <= X <= x + 4]
        boxes = [
            total([box[i * W + y]] + [win_s[n * W + y] for n in near])
            + step.halo_of(windows, x * W + y)
            for y in range(W)
        ]
        step.back(x, boxes, lambda y: kept[i * W + y], own)
    store_sums(part, step.numer + sums[0:F, :], step.denom + sums[F:F + 8, :])


def whole_kernel(own, ylo, yhi, xlo, xhi, zown, zy, matrix, cent, edge, memb, part, inv_s, win_s):
    step = Step(cent, edge)
    mid, outer = mid_column(own, ylo, yhi), outer_column(xlo, xhi)
    windows = step.near_halo(zown, zy, matrix) + step.far_halo(xlo, xhi, matrix)
    for X in range(E):
        def keep(y, inv, X=X):
            inv_s[(X - 2) * W + y] = inv
        for y, w in enumerate(step.front(X, mid if 2 <= X < W + 2 else outer, keep)):
            win_s[X * W + y] = w
    for x in range(W):
        boxes = [
            total([win_s[X * W + y] for X in range(x, x + 5)]) + step.halo_of(windows, x * W + y)
            for y in range(W)
        ]
        step.back(x, boxes, lambda y: inv_s[x * W + y], own, memb)
    store_sums(part, step.numer, step.denom)


VMEM = pl.BlockSpec(memory_space=pltpu.VMEM)
ANY = pl.BlockSpec(memory_space=pl.ANY)


def call(kernel, out_shape, in_specs, scratch_shapes, flops, moved, args):
    return pl.pallas_call(
        kernel,
        out_shape=tuple(jax.ShapeDtypeStruct(s, t) for s, t in out_shape),
        in_specs=in_specs,
        out_specs=(VMEM,) * len(out_shape),
        scratch_shapes=scratch_shapes,
        compiler_params=pltpu.CompilerParams(vmem_limit_bytes=24 << 20),
        cost_estimate=pl.CostEstimate(flops=flops, bytes_accessed=moved, transcendentals=0),
    )(*args)


def columns(n, dtype=F32):
    return (n, F, 128), dtype


def prepare(attributes, start):
    return call(
        prepare_kernel, [columns(COLS, BF16), columns(2, BF16), ((9, 128), F32)], [ANY] * 2,
        [pltpu.VMEM(attributes.shape, BF16), pltpu.VMEM(start.shape, F32),
         pltpu.SemaphoreType.DMA((3,))],
        10 ** 6, 1 << 20,
        [pltpu.with_memory_space_constraint(a, pltpu.HBM) for a in (attributes, start)])


def inner_part(own, ylo, yhi, zown, zy, matrix, cent, edge):
    return call(
        inner_kernel, [columns(4 * W), columns(4 * W), ((F + 8, F), F32)], [VMEM] * 8,
        [pltpu.VMEM(*columns(4 * W)), pltpu.VMEM(*columns(COLS))],
        5 * 10 ** 8, 3 << 20, (own, ylo, yhi, zown, zy, matrix, cent, edge))


def outer_part(own, xlo, xhi, matrix, cent, edge, box, kept, sums):
    return call(
        outer_kernel, [((16, 128), BF16)], [VMEM] * 9,
        [pltpu.VMEM(*columns(4 * W))],
        2 * 10 ** 8, 2 << 20, (own, xlo, xhi, matrix, cent, edge, box, kept, sums))[0]


def whole_update(own, ylo, yhi, xlo, xhi, zown, zy, matrix, cent, edge):
    return call(
        whole_kernel, [((F, W, W, 128), F32), ((16, 128), BF16)], [VMEM] * 10,
        [pltpu.VMEM(*columns(COLS)), pltpu.VMEM(*columns(E * W))],
        8 * 10 ** 8, 3 << 20, (own, ylo, yhi, xlo, xhi, zown, zy, matrix, cent, edge))


def both_ways(up, down, axes, count):
    lo = lax.ppermute(up, axes, [(i, (i + 1) % count) for i in range(count)])
    hi = lax.ppermute(down, axes, [((i + 1) % count, i) for i in range(count)])
    return lo, hi


def gather_sum(part, axes, count):
    every = lax.all_to_all(jnp.broadcast_to(part[None], (count,) + part.shape), axes, 0, 0)
    return jnp.sum(every.astype(F32), axis=0)


def total_sums(part):
    part = gather_sum(part[:10].reshape(5, 2, 128), ("core", "gz"), 16)
    return gather_sum(part.reshape(10, 1, 128)[:9], ("gy", "cx"), 16).reshape(9, 128)


def edges():
    gx, gy, gz = lax.axis_index(XS), lax.axis_index("gy"), lax.axis_index("gz")
    row = lax.broadcasted_iota(jnp.int32, (8, 128), 0)
    inside = jnp.zeros((8, 128), jnp.bool_)
    for i, has in enumerate((gx > 0, gx < 7, gy > 0, gy < 3, gz > 0, gz < 7)):
        inside = inside | ((row == i) & has)
    return inside.astype(F32)


def per_device(attributes, start_centroids):
    edge = edges()
    matrix = jnp.asarray(halo_matrix(), BF16)
    lane = lax.broadcasted_iota(jnp.int32, (1, 1, 128), 2)
    own, ends, cent = prepare(attributes, start_centroids)
    grid = own.reshape(W, W, F, 128)
    ylo, yhi = both_ways(
        grid[:, W - 2:].reshape(2 * W, F, 128), grid[:, :2].reshape(2 * W, F, 128), "gy", 4)
    zlo, zhi = both_ways(ends, ends, "gz", 8)
    zown = jnp.where(lane % 4 < 2, zlo, zhi)
    zylo, zyhi = both_ways(zown, zown, "gy", 4)
    zy = jnp.where(lane // 4 % W >= W // 2, zylo, zyhi)

    def x_slice(x, half):
        return jnp.concatenate(
            [own[x * W:x * W + 2 * W], ylo[2 * x:2 * x + 4], yhi[2 * x:2 * x + 4],
             zown[half:half + 1], zy[half:half + 1]])

    xlo, xhi = both_ways(x_slice(W - 2, 1), x_slice(0, 0), XS, 8)

    box, kept, sums = inner_part(own, ylo, yhi, zown, zy, matrix, cent, edge)
    part = outer_part(own, xlo, xhi, matrix, cent, edge, box, kept, sums)
    cent = total_sums(part)
    memb, part = whole_update(own, ylo, yhi, xlo, xhi, zown, zy, matrix, cent, edge)
    cent = total_sums(part)
    numer = cent[:8].reshape(8, 4, F).transpose(1, 0, 2).reshape(F, F)
    return numer / cent[8, :F][:, None], memb


def solution(mesh):
    split = Mesh(np.asarray(mesh.devices).reshape(4, 2, 4, 8), ("cx", "core", "gy", "gz"))
    return jax.shard_map(
        per_device,
        mesh=split,
        in_specs=(P(None, XS, "gy", "gz"), P()),
        out_specs=(P(), P(None, XS, "gy", "gz")),
        check_vma=False,
    )
```

```python
import jax
import jax.numpy as jnp
import numpy as np
from jax import lax
from jax.experimental import pallas as pl
from jax.experimental.pallas import tpu as pltpu
from jax.sharding import Mesh, PartitionSpec as P

F = 32
W = 8
E = W + 4
COLS = W * W
BF16 = jnp.bfloat16
F32 = jnp.float32
XS = ("cx", "core")
OUTER = (0, 1, W - 2, W - 1)
INNER = tuple(range(2, W - 2))
ROWS = (0, 1, W + 2, W + 3)


def tile_columns():
    def beyond(i):
        return i - W if i >= W // 2 else i + W

    own = [(c // W, c % W) for c in range(COLS)]
    ys = [(x, beyond(y)) for x, y in own]
    xs = [(beyond(j // W + (4 if j >= 16 else 0)), j % W) for j in range(32)]
    return own + ys + xs + [(x, beyond(y)) for x, y in xs]


def halo_matrix():
    src = [(x, y, z) for x, y in tile_columns() for z in (-2, -1, 128, 129)]
    dst = [(c // W, c % W, z) for c in range(COLS) for z in (126, 127, 0, 1)]
    gap = np.abs(np.array(src)[:, None, :] - np.array(dst)[None, :, :])
    return (gap <= 2).all(-1).astype(np.float32)


def band_matrix():
    gap = lax.broadcasted_iota(jnp.int32, (128, 128), 0) - lax.broadcasted_iota(jnp.int32, (128, 128), 1)
    return jnp.where(jnp.abs(gap) <= 2, 1.0, 0.0).astype(BF16)


def recip(x):
    return pl.reciprocal(x, approx=True)


def dot_lanes(a, b):
    return lax.dot_general(a, b, (((1,), (1,)), ((), ())), preferred_element_type=F32)


def unpacked_centroids(sums):
    lane = lax.broadcasted_iota(jnp.int32, (8, 128), 1)
    row = lax.broadcasted_iota(jnp.int32, (8, 128), 0)
    denom = jnp.broadcast_to(sums[8:9, :], (8, 128))
    parts = []
    for g in range(4):
        d = jnp.sum(jnp.where(lane == row + 8 * g, denom, 0.0), axis=1, keepdims=True)
        parts.append(sums[0:8, 32 * g:32 * g + 32] / d)
    return jnp.concatenate(parts, axis=0)


def store_sums(part, numer, denom):
    packed = jnp.concatenate([numer[8 * g:8 * g + 8] for g in range(4)], axis=1)
    every = jnp.concatenate([packed, jnp.concatenate([denom] * 4, axis=1)], axis=0)
    for i in range(5):
        part[i] = every[2 * i:2 * i + 2].astype(BF16)


def turned8(v):
    row = lax.broadcasted_iota(jnp.int32, (8, 128), 0)
    v = list(v)
    for s in (4, 2, 1):
        low = (row & s) == 0
        for i in range(8):
            if not i & s:
                a, b = v[i], v[i + s]
                v[i] = jnp.where(low, a, pltpu.roll(b, s, 0))
                v[i + s] = jnp.where(low, pltpu.roll(a, 8 - s, 0), b)
    return v


def prepare_kernel(attr_hbm, start_hbm, own, up, down, ends, cent, attr, start, sems):
    fetch = [
        pltpu.make_async_copy(attr_hbm.at[:, x:x + 4], attr.at[:, x:x + 4], sems.at[x // 4])
        for x in range(0, W, 4)
    ]
    fetch.append(pltpu.make_async_copy(start_hbm, start, sems.at[2]))
    for f in fetch:
        f.start()
    lane = lax.broadcasted_iota(jnp.int32, (1, 128), 1) // 4
    for half in range(2):
        acc = jnp.zeros((F, 128), F32)
        fetch[half].wait()
        for x in range(half * 4, half * 4 + 4):
            wide = [attr[a, x].astype(F32) for a in range(F)]
            groups = [turned8(wide[8 * g:8 * g + 8]) for g in range(4)]
            for y in range(W):
                c = x * W + y
                j = c % 32
                col = jnp.concatenate([groups[g][y] for g in range(4)], axis=0)
                own[c] = col.astype(BF16)
                if y < 2:
                    down[x * 2 + y] = col.astype(BF16)
                elif y >= W - 2:
                    up[x * 2 + y - W + 2] = col.astype(BF16)
                acc = jnp.where(lane == j, pltpu.roll(col, (4 * j + 2) % 128, 1), acc)
        ends[half] = acc.astype(BF16)
    fetch[-1].wait()
    cent[0:8, :] = jnp.concatenate([start[8 * g:8 * g + 8, :] for g in range(4)], axis=1)
    cent[8:9, :] = jnp.ones((1, 128), F32)


class Step:
    def __init__(self, cent, edge):
        c = unpacked_centroids(cent)
        self.cbm2 = (-2.0 * c.astype(BF16).astype(F32)).astype(BF16)
        self.csq1 = jnp.broadcast_to(jnp.sum(c * c, axis=1, keepdims=True) + 1.0, (F, 128))
        self.xlo, self.xhi, self.ylo, self.yhi, self.zlo, self.zhi = [edge[i:i + 1, :] for i in range(6)]
        self.band = band_matrix()
        self.lane = lax.broadcasted_iota(jnp.int32, (1, 128), 1)
        self.numer = jnp.zeros((F, F), F32)
        self.ends = jnp.where((self.lane < 2) | (self.lane >= 126), 1.0, 0.0)
        self.denom = jnp.zeros((8, F), F32)

    def inverse(self, a):
        af = a.astype(F32)
        sq = jnp.sum(af * af, axis=0, keepdims=True)
        cross = jnp.dot(self.cbm2, a, preferred_element_type=F32)
        return [
            recip(cross[:, s:s + 128] + self.csq1 + sq[:, s:s + 128])
            for s in range(0, a.shape[1], 128)
        ]

    def normalised(self, inv, mask):
        scale = recip(jnp.sum(inv, axis=0, keepdims=True))
        if mask is not None:
            scale = scale * mask
        return (inv * scale).astype(BF16)

    def front(self, X, column, keep):
        mx = self.xlo if X < 2 else (self.xhi if X >= W + 2 else None)
        rounded = []
        for Y in range(0, E, 2):
            my = self.ylo if Y < 2 else (self.yhi if Y >= W + 2 else None)
            m = mx if my is None else (my if mx is None else mx * my)
            pair = jnp.concatenate([column(X, Y), column(X, Y + 1)], axis=1)
            for i, inv in enumerate(self.inverse(pair)):
                if mx is None and my is None:
                    keep(Y + i - 2, inv)
                rounded.append(self.normalised(inv, m))
        z = jnp.dot(jnp.concatenate(rounded, axis=0), self.band, preferred_element_type=F32)
        cols = [z[F * Y:F * Y + F] for Y in range(E)]
        p = [cols[Y] + cols[Y + 1] for Y in range(E - 1)]
        return [p[y] + p[y + 2] + cols[y + 4] for y in range(W)]

    def halo(self, tiles, matrix, near):
        j = self.lane // 4
        mz = jnp.where(self.lane % 4 < 2, self.zlo, self.zhi)
        my = mz * jnp.where(j % W >= W // 2, self.ylo, self.yhi)
        mx = jnp.where(j >= 16, self.xlo, self.xhi)
        masks = [mz, mz, my, my] if near else [mz * mx, my * mx]
        rounded = []
        for i in range(0, len(tiles), 2):
            pair = jnp.concatenate([tiles[i], tiles[i + 1]], axis=1)
            for inv, m in zip(self.inverse(pair), masks[i:i + 2]):
                rounded.append(self.normalised(inv, m))
        return jnp.dot(jnp.concatenate(rounded, axis=1), matrix, preferred_element_type=F32)

    def near_halo(self, zown, zy, matrix):
        return self.halo([zown[0], zown[1], zy[0], zy[1]], matrix[0:4 * 128, :], True)

    def far_halo(self, xlo, xhi, matrix):
        tiles = [jnp.where(self.lane >= 64, xlo[2 * E + i].astype(F32), xhi[2 * E + i].astype(F32)).astype(BF16)
                 for i in range(2)]
        return self.halo(tiles, matrix[4 * 128:6 * 128, :], False)

    def halo_of(self, windows, c):
        half = windows[:, c // 32 * 128:c // 32 * 128 + 128]
        turned = pltpu.roll(half, (126 - 4 * (c % 32)) % 128, 1)
        return turned * self.ends

    def back(self, x, boxes, inv, own, memb=None):
        ws, ms = [], []
        for y in range(W):
            prod = inv(y) * boxes[y]
            m = prod * recip(jnp.sum(prod, axis=0, keepdims=True))
            ms.append(m)
            ws.append((m * m).astype(BF16))
        if memb is not None:
            for g in range(4):
                for k, rows in enumerate(turned8([m[8 * g:8 * g + 8] for m in ms])):
                    memb[8 * g + k, x] = rows
        w = jnp.concatenate(ws, axis=1)
        t = jnp.concatenate([own[x * W + y] for y in range(W)], axis=1)
        self.numer = self.numer + dot_lanes(w, t)
        self.denom = self.denom + dot_lanes(jnp.ones((8, W * 128), BF16), w)


def total(arrays):
    out = arrays[0]
    for a in arrays[1:]:
        out = out + a
    return out


def mid_column(own, ylo, yhi):
    def column(X, Y):
        x = X - 2
        if Y < 2:
            return ylo[x * 2 + Y]
        if Y >= W + 2:
            return yhi[x * 2 + Y - W - 2]
        return own[x * W + Y - 2]
    return column


def outer_column(xlo, xhi):
    def column(X, Y):
        ref, i = (xlo, X) if X < 2 else (xhi, X - W - 2)
        if Y < 2:
            return ref[16 + i * 2 + Y]
        if Y >= W + 2:
            return ref[20 + i * 2 + Y - W - 2]
        return ref[i * W + Y - 2]
    return column


def inner_kernel(own, ylo, yhi, zown, zy, matrix, cent, edge, box, kept, sums, inv_s, win_s):
    step = Step(cent, edge)
    column = mid_column(own, ylo, yhi)
    windows = step.near_halo(zown, zy, matrix)
    for x in range(W):
        def keep(y, inv, x=x):
            if x in INNER:
                inv_s[(x - 2) * W + y] = inv
            else:
                kept[OUTER.index(x) * W + y] = inv
        for y, w in enumerate(step.front(x + 2, column, keep)):
            win_s[x * W + y] = w

    def mid_box(x, y):
        rows = range(max(x - 2, 0), min(x + 3, W))
        return total([win_s[r * W + y] for r in rows]) + step.halo_of(windows, x * W + y)

    for x in INNER:
        step.back(x, [mid_box(x, y) for y in range(W)], lambda y: inv_s[(x - 2) * W + y], own)
    for i, x in enumerate(OUTER):
        for y in range(W):
            box[i * W + y] = mid_box(x, y)
    sums[0:F, :] = step.numer
    sums[F:F + 8, :] = step.denom


def outer_kernel(own, xlo, xhi, matrix, cent, edge, box, kept, sums, part, win_s):
    step = Step(cent, edge)
    column = outer_column(xlo, xhi)
    windows = step.far_halo(xlo, xhi, matrix)
    for i, X in enumerate(ROWS):
        for y, w in enumerate(step.front(X, column, None)):
            win_s[i * W + y] = w
    for i, x in enumerate(OUTER):
        near = [n for n, X in enumerate(ROWS) if x <= X <= x + 4]
        boxes = [
            total([box[i * W + y]] + [win_s[n * W + y] for n in near])
            + step.halo_of(windows, x * W + y)
            for y in range(W)
        ]
        step.back(x, boxes, lambda y: kept[i * W + y], own)
    store_sums(part, step.numer + sums[0:F, :], step.denom + sums[F:F + 8, :])


def whole_kernel(own, ylo, yhi, xlo, xhi, zown, zy, matrix, cent, edge, memb, part, inv_s, win_s):
    step = Step(cent, edge)
    mid, outer = mid_column(own, ylo, yhi), outer_column(xlo, xhi)
    windows = step.near_halo(zown, zy, matrix) + step.far_halo(xlo, xhi, matrix)
    for X in range(E):
        def keep(y, inv, X=X):
            inv_s[(X - 2) * W + y] = inv
        for y, w in enumerate(step.front(X, mid if 2 <= X < W + 2 else outer, keep)):
            win_s[X * W + y] = w
    for x in range(W):
        boxes = [
            total([win_s[X * W + y] for X in range(x, x + 5)]) + step.halo_of(windows, x * W + y)
            for y in range(W)
        ]
        step.back(x, boxes, lambda y: inv_s[x * W + y], own, memb)
    store_sums(part, step.numer, step.denom)


VMEM = pl.BlockSpec(memory_space=pltpu.VMEM)
ANY = pl.BlockSpec(memory_space=pl.ANY)


def call(kernel, out_shape, in_specs, scratch_shapes, flops, moved, args):
    return pl.pallas_call(
        kernel,
        out_shape=tuple(jax.ShapeDtypeStruct(s, t) for s, t in out_shape),
        in_specs=in_specs,
        out_specs=(VMEM,) * len(out_shape),
        scratch_shapes=scratch_shapes,
        compiler_params=pltpu.CompilerParams(vmem_limit_bytes=24 << 20),
        cost_estimate=pl.CostEstimate(flops=flops, bytes_accessed=moved, transcendentals=0),
    )(*args)


def columns(n, dtype=F32):
    return (n, F, 128), dtype


def prepare(attributes, start):
    return call(
        prepare_kernel, [columns(COLS, BF16), columns(2 * W, BF16), columns(2 * W, BF16), columns(2, BF16), ((9, 128), F32)], [ANY] * 2,
        [pltpu.VMEM(attributes.shape, BF16), pltpu.VMEM(start.shape, F32),
         pltpu.SemaphoreType.DMA((3,))],
        10 ** 6, 1 << 20,
        [pltpu.with_memory_space_constraint(a, pltpu.HBM) for a in (attributes, start)])


def inner_part(own, ylo, yhi, zown, zy, matrix, cent, edge):
    return call(
        inner_kernel, [columns(4 * W), columns(4 * W), ((F + 8, F), F32)], [VMEM] * 8,
        [pltpu.VMEM(*columns(4 * W)), pltpu.VMEM(*columns(COLS))],
        5 * 10 ** 8, 3 << 20, (own, ylo, yhi, zown, zy, matrix, cent, edge))


def outer_part(own, xlo, xhi, matrix, cent, edge, box, kept, sums):
    return call(
        outer_kernel, [((5, 2, 128), BF16)], [VMEM] * 9,
        [pltpu.VMEM(*columns(4 * W))],
        2 * 10 ** 8, 2 << 20, (own, xlo, xhi, matrix, cent, edge, box, kept, sums))[0]


def whole_update(own, ylo, yhi, xlo, xhi, zown, zy, matrix, cent, edge):
    return call(
        whole_kernel, [((F, W, W, 128), F32), ((5, 2, 128), BF16)], [VMEM] * 10,
        [pltpu.VMEM(*columns(COLS)), pltpu.VMEM(*columns(E * W))],
        8 * 10 ** 8, 3 << 20, (own, ylo, yhi, xlo, xhi, zown, zy, matrix, cent, edge))


def both_ways(up, down, axes, count):
    lo = lax.ppermute(up, axes, [(i, (i + 1) % count) for i in range(count)])
    hi = lax.ppermute(down, axes, [((i + 1) % count, i) for i in range(count)])
    return lo, hi


def gather_sum(part, axes, count):
    every = lax.all_to_all(jnp.broadcast_to(part[None], (count,) + part.shape), axes, 0, 0)
    return jnp.sum(every.astype(F32), axis=0)


def total_sums(part):
    part = gather_sum(part, ("core", "gz"), 16)
    return gather_sum(part.reshape(10, 1, 128)[:9], ("cx", "gy"), 16).reshape(9, 128)


def edges():
    gx, gy, gz = lax.axis_index(XS), lax.axis_index("gy"), lax.axis_index("gz")
    row = lax.broadcasted_iota(jnp.int32, (8, 128), 0)
    inside = jnp.zeros((8, 128), jnp.bool_)
    for i, has in enumerate((gx > 0, gx < 7, gy > 0, gy < 3, gz > 0, gz < 7)):
        inside = inside | ((row == i) & has)
    return inside.astype(F32)


def per_device(attributes, start_centroids):
    edge = edges()
    matrix = jnp.asarray(halo_matrix(), BF16)
    lane = lax.broadcasted_iota(jnp.int32, (1, 1, 128), 2)
    own, up, down, ends, cent = prepare(attributes, start_centroids)
    ylo, yhi = both_ways(up, down, "gy", 4)
    zlo, zhi = both_ways(ends, ends, "gz", 8)
    zown = jnp.where(lane % 4 < 2, zlo, zhi)
    zylo, zyhi = both_ways(zown, zown, "gy", 4)
    zy = jnp.where(lane // 4 % W >= W // 2, zylo, zyhi)

    def x_slice(x, half):
        return jnp.concatenate(
            [own[x * W:x * W + 2 * W], ylo[2 * x:2 * x + 4], yhi[2 * x:2 * x + 4],
             zown[half:half + 1], zy[half:half + 1]])

    xlo, xhi = both_ways(x_slice(W - 2, 1), x_slice(0, 0), XS, 8)

    box, kept, sums = inner_part(own, ylo, yhi, zown, zy, matrix, cent, edge)
    part = outer_part(own, xlo, xhi, matrix, cent, edge, box, kept, sums)
    cent = total_sums(part)
    memb, part = whole_update(own, ylo, yhi, xlo, xhi, zown, zy, matrix, cent, edge)
    cent = total_sums(part)
    numer = cent[:8].reshape(8, 4, F).transpose(1, 0, 2).reshape(F, F)
    return numer / cent[8, :F][:, None], memb


def solution(mesh):
    split = Mesh(np.asarray(mesh.devices).reshape(4, 2, 4, 8), ("cx", "core", "gy", "gz"))
    return jax.shard_map(
        per_device,
        mesh=split,
        in_specs=(P(None, XS, "gy", "gz"), P()),
        out_specs=(P(), P(None, XS, "gy", "gz")),
        check_vma=False,
    )
```
